512 devices in a mesh: seq: 128 (over z, x, core), mp: 4 (over y).
Axes of the slice: x: 4, y: 4, z: 16, core: 2. Of those that a mesh axis runs over, the one named last changes fastest.
Arguments:
- queries: bfloat16 [16384, 4096], P(('seq', 'mp')), may hold values from -120 to 120
- keys: bfloat16 [16384, 4096], P(('seq', 'mp')), may hold values from -6 to 6
- values: bfloat16 [16384, 4096], P(('seq', 'mp')), may hold values from -6 to 6
- text_queries: bfloat16 [16384, 4096], P(('seq', 'mp')), may hold values from -6 to 6
- text_states: bfloat16 [2, 128, 300, 4096], P(None, 'seq', None, 'mp'), may hold values from -6 to 6
- packed_pos: int32 [16384], P('seq'), may hold values from 0 to 16383, as said below
- image_of: int32 [16384], P('seq'), may hold values from 0 to 127, as said below
Outputs:
- attended: bfloat16 [16384, 4096], P('seq', 'mp')
The draws below stay inside these ranges and needn't reach their ends.
Inputs may be any that keep to these rules, and one draw needn't show every extreme that they name: packed_pos is a permutation; the rows that one index of seq holds send exactly 128 // 128 rows to the packed rows of each index of seq (packed rows k * 128 to (k+1) * 128 - 1 belong to index k). `image_of`: ids never fall along the rows and every image has rows; the rows of image i lie within the packed rows of the seq indices i and i + 1.
All inputs are finite; a program needn't handle non-finite values.
Results may differ from the reference program's by a relative error of at most 0.0049.
Values may be sent and summed in bfloat16 or wider, within the bound.
A program may use at most 64 MiB of HBM per device.

```python
import math
import jax
import jax.numpy as jnp
from jax import lax

HEADS = 32
HD = 128
TOK_DEV = 128
TXT = 300
IMG_DEV = 1
FEAT = 4096
TOKENS = 16384
IMAGES = 128


def shared_rows(key):
    return jnp.clip(jax.random.normal(key, (TOKENS, HEADS * HD), jnp.float32), -6.0, 6.0)


def draw_keys(key, part):
    base = shared_rows(key)
    return base.astype(jnp.bfloat16)


def draw_queries(key, part):
    base = shared_rows(key)
    key = jax.random.fold_in(key, 3)
    first = jax.random.fold_in(key, 0)
    return jnp.clip(jax.random.normal(first, base.shape, jnp.float32), -6.0, 6.0).astype(jnp.bfloat16)


def draw_packed_pos(key, part):
    key = jax.random.fold_in(key, 11)
    devices = TOKENS // TOK_DEV
    capacity = TOK_DEV // devices
    first, second = jax.random.split(key)
    source_order = jax.vmap(lambda k: jax.random.permutation(k, TOK_DEV))(jax.random.split(first, devices))
    target_order = jax.vmap(lambda k: jax.random.permutation(k, TOK_DEV))(jax.random.split(second, devices))
    source = jnp.arange(devices, dtype=jnp.int32)[:, None, None]
    target = jnp.arange(devices, dtype=jnp.int32)[None, :, None]
    within = jnp.arange(capacity, dtype=jnp.int32)[None, None, :]
    arrival = source * TOK_DEV + source_order[source, target * capacity + within]
    landing = target * TOK_DEV + target_order[target, source * capacity + within]
    result = jnp.zeros((TOKENS,), jnp.int32).at[arrival.reshape(-1)].set(landing.reshape(-1).astype(jnp.int32))
    return result


def draw_image_of(key, part):
    key = jax.random.fold_in(key, 17)
    devices = TOKENS // TOK_DEV
    first, second = jax.random.split(key)
    offsets = jax.random.randint(first, (devices,), 0, TOK_DEV).astype(jnp.int32)
    offsets = offsets.at[0].set(0)
    starts = jnp.arange(devices, dtype=jnp.int32) * TOK_DEV + offsets
    ends = jnp.concatenate([starts[1:], jnp.array([TOKENS], jnp.int32)])
    cuts = jax.random.randint(second, (devices, IMG_DEV - 1), starts[:, None] + 1, ends[:, None]).astype(jnp.int32)
    cuts = jnp.sort(cuts, axis=1)
    position = jnp.arange(TOKENS, dtype=jnp.int32)
    group = jnp.sum((position[:, None] >= starts[None, :]).astype(jnp.int32), axis=1) - 1
    inside = jnp.sum((position[:, None] >= cuts[group]).astype(jnp.int32), axis=1)
    return (group * IMG_DEV + inside).astype(jnp.int32)


def steps_of(own_key, dims, pieces, low, largest):
    level, own = 1.0, jax.random.fold_in(own_key, 6)
    for dim, parts in pieces:
        steps = jnp.exp(jax.random.uniform(jax.random.fold_in(own, dim), (parts,), jnp.float32, low / len(pieces), largest / len(pieces)))
        level = level * jnp.repeat(steps, dims[dim] // parts).reshape([-1 if axis == dim else 1 for axis in range(len(dims))])
    return level


def noise(key, extent, spread, limit, cuts=(), kind=jnp.bfloat16):
    values = jax.random.normal(key, extent, jnp.float32) * spread
    if len(cuts) > 0:
        values = steps_of(key, extent, cuts, -0.22, 0.18) * values
    return jnp.clip(values, min=-limit, max=limit).astype(kind)


def setup_inputs(seed: int = 0) -> dict:
    key_of = jax.random.split(jax.random.key(seed), 8)
    queries = draw_queries(jax.random.fold_in(key_of[7], 71), 0)
    keys = draw_keys(jax.random.fold_in(key_of[7], 71), 0)
    values = noise(key_of[2], (TOKENS, FEAT), 1.0, 6.0, ((0, 512),))
    text_queries = noise(key_of[3], (TOKENS, FEAT), 1.0, 6.0, ((0, 512),))
    text_states = noise(key_of[4], (2, IMAGES, TXT, FEAT), 1.0, 6.0, ((1, 128), (3, 4)))
    packed_pos = draw_packed_pos(jax.random.fold_in(key_of[7], 71), 0)
    image_of = draw_image_of(jax.random.fold_in(key_of[7], 71), 0)
    return {"queries": queries, "keys": keys, "values": values, "text_queries": text_queries, "text_states": text_states, "packed_pos": packed_pos, "image_of": image_of}


def attend(query, key_rows, value_rows, mask):
    scale = 1.0 / math.sqrt(HD)
    scores = jnp.einsum('qhd,khd->hqk', query, key_rows) * scale
    scores = jnp.where(mask[None], scores, -1e+30)
    top = lax.optimization_barrier(jnp.max(scores, axis=2, keepdims=True))
    expo = jnp.exp(scores - top)
    weights = (expo / lax.optimization_barrier(jnp.sum(expo, axis=2, keepdims=True))).astype(jnp.bfloat16)
    weights = lax.optimization_barrier(weights).astype(jnp.float32)
    return jnp.einsum('hqk,khd->qhd', weights, value_rows)

def reference(queries, keys, values, text_queries, text_states, packed_pos, image_of):
    stacked = jnp.stack([queries, keys, values, text_queries])
    packed = jnp.zeros_like(stacked).at[:, packed_pos].set(stacked)
    blocks = TOKENS // TOK_DEV
    padded = jnp.pad(packed[1:3], ((0, 0), (TOK_DEV, TOK_DEV), (0, 0)))
    padded_ids = jnp.pad(image_of + 1, (TOK_DEV, TOK_DEV))
    span = IMG_DEV * TXT

    def one_block(index):
        start = (index * TOK_DEV).astype(jnp.int32)
        query = lax.dynamic_slice_in_dim(packed[0], start, TOK_DEV, 0).reshape(TOK_DEV, HEADS, HD).astype(jnp.float32)
        cross_query = lax.dynamic_slice_in_dim(packed[3], start, TOK_DEV, 0).reshape(TOK_DEV, HEADS, HD).astype(jnp.float32)
        nearby = lax.dynamic_slice_in_dim(padded, start, 3 * TOK_DEV, 1).reshape(2, 3 * TOK_DEV, HEADS, HD).astype(jnp.float32)
        near_ids = lax.dynamic_slice_in_dim(padded_ids, start, 3 * TOK_DEV, 0)
        own_ids = lax.dynamic_slice_in_dim(image_of, start, TOK_DEV, 0)
        self_out = attend(query, nearby[0], nearby[1], (own_ids + 1)[:, None] == near_ids[None, :])
        earlier_start = (jnp.maximum(index - 1, 0) * IMG_DEV).astype(jnp.int32)
        own_start = (index * IMG_DEV).astype(jnp.int32)
        earlier = lax.dynamic_slice_in_dim(text_states, earlier_start, IMG_DEV, 1)
        current = lax.dynamic_slice_in_dim(text_states, own_start, IMG_DEV, 1)
        chosen = jnp.concatenate([earlier, current], axis=1).reshape(2, 2 * span, HEADS, HD).astype(jnp.float32)
        chosen_ids = (index - 1) * IMG_DEV + jnp.arange(2 * span, dtype=jnp.int32) // TXT
        cross_out = attend(cross_query, chosen[0], chosen[1], own_ids[:, None] == chosen_ids[None, :])
        return (self_out + cross_out).reshape(TOK_DEV, HEADS * HD).astype(jnp.bfloat16)
    result = lax.map(one_block, jnp.arange(blocks, dtype=jnp.int32))
    return result.reshape(TOKENS, HEADS * HD)
```

```python
import functools
import math

import jax
import jax.numpy as jnp
from jax import lax
from jax.experimental import pallas as pl
from jax.experimental.pallas import tpu as pltpu
from jax.sharding import PartitionSpec as P

MESH = pl.DeviceIdType.MESH
HD = 128
ROWS = 128
NZ = 16
NW = 8
NY = 4
FEAT = 1024
HEADS = 8
TXT = 300
Q, K, V, T = 0, 1, 2, 3
CHUNKS = ((K, 0, 1024), (V, 0, 1024), (T, 0, 1024), (Q, 0, 512), (Q, 512, 512))
NC = len(CHUNKS)
F32 = jnp.float32
BF16 = jnp.bfloat16
I32 = jnp.int32


def iota(shape, dim):
    return lax.broadcasted_iota(I32, shape, dim)


def one_hot(condition):
    return jnp.where(condition, 1.0, 0.0).astype(BF16)


def dot(a, b):
    return jnp.dot(a, b, preferred_element_type=F32)


def dot_t(a, b):
    return lax.dot_general(a, b, (((1,), (1,)), ((), ())), preferred_element_type=F32)


def kernel(q_ref, k_ref, v_ref, t_ref, text_ref, pos_ref, img_ref, o_ref, *scratch):
    scratch = list(scratch)
    take = lambda n: [scratch.pop(0) for _ in range(n)]
    ybuf, zsend, zrecv, xsend, xrecv = (take(NC) for _ in range(5))
    (packed, kv_prev, kv_next, txt, cross, slot_send, slot_recv, row_send, row_recv, img_near) = take(10)
    (local_sem, y_ssem, y_rsem, z_ssem, z_rsem, x_ssem, x_rsem, n_ssem, n_rsem, t_ssem, t_rsem, s_sems, i_sems) = take(13)
    arrays = (q_ref, k_ref, v_ref, t_ref)

    me = lax.axis_index("seq")
    y = lax.axis_index("mp")
    z, w = me // NW, me % NW
    z_device = lambda other: {"seq": other * NW + w}
    w_device = lambda other: {"seq": z * NW + other}
    after = {"seq": lax.rem(me + 1, NZ * NW)}
    before = {"seq": lax.rem(me + NZ * NW - 1, NZ * NW)}

    def remote(src, dst, send, recv, device):
        return pltpu.make_async_remote_copy(
            src_ref=src, dst_ref=dst, send_sem=send, recv_sem=recv, device_id=device, device_id_type=MESH
        )

    def bytes_of(ref, send, recv):
        return remote(ref, ref, send, recv, after)

    barrier = pltpu.get_barrier_semaphore()
    for i in range(1, NY):
        pl.semaphore_signal(barrier, inc=1, device_id={"mp": lax.rem(y + i, NY)}, device_id_type=MESH)

    def greet_z(i, carry):
        pl.semaphore_signal(barrier, inc=1, device_id=z_device(lax.rem(z + i, NZ)), device_id_type=MESH)
        return carry

    lax.fori_loop(1, NZ, greet_z, 0)

    def greet_w(i, carry):
        pl.semaphore_signal(barrier, inc=1, device_id=w_device(lax.rem(w + i, NW)), device_id_type=MESH)
        return carry

    lax.fori_loop(1, NW, greet_w, 0)
    for device in (after, before):
        pl.semaphore_signal(barrier, inc=1, device_id=device, device_id_type=MESH)

    own = []
    for c, (a, first, columns) in enumerate(CHUNKS):
        start = pl.multiple_of(y * FEAT + first, 128)
        own.append(
            pltpu.make_async_copy(
                arrays[a].at[:, pl.ds(start, columns)], ybuf[c].at[pl.ds(pl.multiple_of(y * 32, 32), 32)], local_sem.at[c]
            )
        )
        own[-1].start()
    own_text = pltpu.make_async_copy(text_ref, txt.at[1], local_sem.at[NC])
    own_text.start()

    pos = pos_ref[...]
    target = lax.shift_right_logical(pos, 7)
    slot = pos & (ROWS - 1)
    image = img_ref[...]
    out_row = iota((2 * ROWS, ROWS), 0)
    same = (lax.shift_right_logical(out_row, 4) * NW + (out_row & 7)) == target
    right_half = (out_row & 8) == 8
    send_left = one_hot(same & ~right_half)
    send_right = one_hot(same & right_half)
    to_z = one_hot(iota((NZ, ROWS), 0) == lax.shift_right_logical(target, 3))
    lane_of = (target & 7) * NZ + z
    by_lane = jnp.where(iota((ROWS, ROWS), 0) == lane_of, slot.astype(F32), 0.0).astype(BF16)
    slots = dot_t(to_z, by_lane).astype(I32)
    for i in range(NZ):
        slot_send[i] = slots[i : i + 1]

    pl.semaphore_wait(barrier, NY - 1 + NZ - 1 + NW - 1 + 2)

    for c, (a, first, columns) in enumerate(CHUNKS):
        for i in range(1, NY):
            other = lax.rem(y + i, NY)
            start = pl.multiple_of(other * FEAT + first, 128)
            remote(
                arrays[a].at[:, pl.ds(start, columns)],
                ybuf[c].at[pl.ds(pl.multiple_of(y * 32, 32), 32)],
                y_ssem.at[c],
                y_rsem.at[c],
                {"mp": other},
            ).start()

    def far_first(i):
        return lax.rem(z + 8 + jnp.where(i % 2 == 0, -(i // 2), i // 2), NZ)

    def send_slots(i, carry):
        to = far_first(i)
        remote(slot_send.at[to], slot_recv.at[z], s_sems.at[0], s_sems.at[1], z_device(to)).start()
        return carry

    lax.fori_loop(1, NZ, send_slots, 0)
    slot_recv[z] = slot_send[z]
    remote(img_ref, img_near.at[0], i_sems.at[0], i_sems.at[1], after).start()
    remote(img_ref, img_near.at[1], i_sems.at[2], i_sems.at[3], before).start()

    for c, (a, first, columns) in enumerate(CHUNKS):
        half = columns // 2
        own[c].wait()
        bytes_of(ybuf[c].at[pl.ds(0, 96)], y_ssem.at[c], y_rsem.at[c]).wait_recv()
        out = dot(send_left, ybuf[c][:, :half]) + dot(send_right, ybuf[c][:, half:])
        zsend[c][...] = out.astype(BF16).reshape(NZ, 16, half)

        def send_z(i, carry):
            to = far_first(i)
            remote(zsend[c].at[to], zrecv[c].at[z], z_ssem.at[c], z_rsem.at[c], z_device(to)).start()
            return carry

        lax.fori_loop(1, NZ, send_z, 0)
        zrecv[c][z] = zsend[c][z]
        if c == 0:
            for i in range(2):
                remote(text_ref.at[i], txt.at[0, i], t_ssem.at[i], t_rsem.at[i], after).start()

    bytes_of(slot_recv.at[pl.ds(0, NZ - 1)], s_sems.at[0], s_sems.at[1]).wait_recv()
    row = slot_recv[0]
    for i in range(1, NZ):
        row = row + slot_recv[i]
    row_send[...] = row

    def send_row(i, carry):
        to = lax.rem(w + i, NW)
        remote(row_send, row_recv.at[w], s_sems.at[2], s_sems.at[3], w_device(to)).start()
        return carry

    lax.fori_loop(1, NW, send_row, 0)
    row_recv[w] = row
    bytes_of(row_recv.at[pl.ds(0, NW - 1)], s_sems.at[2], s_sems.at[3]).wait_recv()
    rows = jnp.concatenate([row_recv[i] for i in range(NW)], axis=0)
    pick = one_hot(iota((ROWS, ROWS), 0) == w * NZ + (iota((ROWS, ROWS), 1) & (NZ - 1)))
    landed = dot(rows.astype(F32).astype(BF16), pick)
    mine = lax.shift_right_logical(iota((NW, ROWS), 1), 4) == iota((NW, ROWS), 0)
    landing = jnp.sum(jnp.where(mine, landed, 0.0), axis=0, keepdims=True).astype(I32)
    place = one_hot(iota((ROWS, ROWS), 0) == landing)

    count = lambda flags: jnp.sum(jnp.where(flags, 1.0, 0.0), axis=1, keepdims=True).astype(I32)
    for i in range(2):
        bytes_of(img_near.at[i], i_sems.at[2 * i], i_sems.at[2 * i + 1]).wait_recv()
    cut = count(image < me)
    cut_prev = count(img_near[0] < me - 1)
    cut_next = count(img_near[1] == me)
    query_row, key_row = iota((ROWS, ROWS), 0), iota((ROWS, ROWS), 1)
    earlier = query_row < cut
    mask_own = earlier == (key_row < cut)
    mask_near = (earlier & (key_row >= cut_prev)) | (~earlier & (key_row < cut_next))
    earlier_text = iota((ROWS, TXT), 0) < cut
    scale = math.log2(math.e) / math.sqrt(HD)

    mid_row, mid_col = iota((ROWS, 2 * ROWS), 0), iota((ROWS, 2 * ROWS), 1)
    from_row = (mid_row & (NZ - 1)) * 16 + lax.shift_right_logical(mid_row, 4)
    mid_left = one_hot(mid_col == from_row)
    mid_right = one_hot(mid_col == from_row + 8)

    def cross_head(h, carry):
        cols = pl.ds(pl.multiple_of(h * HD, HD), HD)
        query = packed[T, :, cols]
        scores = jnp.where(
            earlier_text, dot_t(query, txt[0, 0, 0, :, cols]), dot_t(query, txt[1, 0, 0, :, cols])
        )
        top = jnp.max(scores, axis=1, keepdims=True)
        expo = jnp.exp2((scores - top) * scale)
        total = jnp.sum(expo, axis=1, keepdims=True)
        weights = expo.astype(BF16)
        out = jnp.where(
            earlier, dot(weights, txt[0, 1, 0, :, cols]), dot(weights, txt[1, 1, 0, :, cols])
        )
        cross[:, cols] = out / total
        return carry

    def self_head(h, carry):
        cols = pl.ds(pl.multiple_of(h * HD, HD), HD)
        query = packed[Q, :, cols]
        own_scores = jnp.where(mask_own, dot_t(query, packed[K, :, cols]), -1e30)
        near = jnp.where(earlier, dot_t(query, kv_prev[0, :, cols]), dot_t(query, kv_next[0, :, cols]))
        near = jnp.where(mask_near, near, -1e30)
        top = jnp.max(jnp.maximum(own_scores, near), axis=1, keepdims=True)
        own_expo = jnp.exp2((own_scores - top) * scale)
        near_expo = jnp.exp2((near - top) * scale)
        total = jnp.sum(own_expo + near_expo, axis=1, keepdims=True)
        near_weights = near_expo.astype(BF16)
        out = dot(own_expo.astype(BF16), packed[V, :, cols])
        out = out + jnp.where(
            earlier, dot(near_weights, kv_prev[1, :, cols]), dot(near_weights, kv_next[1, :, cols])
        )
        o_ref[:, cols] = (out / total + cross[:, cols]).astype(BF16)
        return carry

    for c, (a, first, columns) in enumerate(CHUNKS):
        half = columns // 2
        bytes_of(zrecv[c].at[pl.ds(0, NZ - 1)], z_ssem.at[c], z_rsem.at[c]).wait_recv()
        arrived = zrecv[c][...].reshape(2 * ROWS, half)
        xsend[c][:, :, :half] = dot(mid_left, arrived).astype(BF16).reshape(NW, NZ, half)
        xsend[c][:, :, half:] = dot(mid_right, arrived).astype(BF16).reshape(NW, NZ, half)

        def send_x(i, carry):
            to = lax.rem(w + i, NW)
            remote(xsend[c].at[to], xrecv[c].at[w], x_ssem.at[c], x_rsem.at[c], w_device(to)).start()
            return carry

        lax.fori_loop(1, NW, send_x, 0)
        xrecv[c][w] = xsend[c][w]
        bytes_of(xrecv[c].at[pl.ds(0, NW - 1)], x_ssem.at[c], x_rsem.at[c]).wait_recv()
        packed[a, :, first : first + columns] = dot(place, xrecv[c][...].reshape(ROWS, columns)).astype(BF16)
        if a in (K, V):
            i = a - K
            remote(packed.at[a], kv_prev.at[i], n_ssem.at[2 * i], n_rsem.at[2 * i], after).start()
            remote(packed.at[a], kv_next.at[i], n_ssem.at[2 * i + 1], n_rsem.at[2 * i + 1], before).start()
        elif a == T:
            own_text.wait()
            for i in range(2):
                bytes_of(txt.at[0, i], t_ssem.at[i], t_rsem.at[i]).wait_recv()
            lax.fori_loop(0, HEADS, cross_head, 0)
        else:
            if first == 0:
                for i in range(2):
                    bytes_of(kv_prev.at[i], n_ssem.at[2 * i], n_rsem.at[2 * i]).wait_recv()
                    bytes_of(kv_next.at[i], n_ssem.at[2 * i + 1], n_rsem.at[2 * i + 1]).wait_recv()
            lax.fori_loop(first // HD, (first + columns) // HD, self_head, 0)

    bytes_of(slot_send.at[pl.ds(0, NZ - 1)], s_sems.at[0], s_sems.at[1]).wait_send()
    bytes_of(row_recv.at[pl.ds(0, NW - 1)], s_sems.at[2], s_sems.at[3]).wait_send()
    for i in range(2):
        bytes_of(img_near.at[i], i_sems.at[2 * i], i_sems.at[2 * i + 1]).wait_send()
        bytes_of(txt.at[0, i], t_ssem.at[i], t_rsem.at[i]).wait_send()
        bytes_of(kv_prev.at[i], n_ssem.at[2 * i], n_rsem.at[2 * i]).wait_send()
        bytes_of(kv_next.at[i], n_ssem.at[2 * i + 1], n_rsem.at[2 * i + 1]).wait_send()
    for c in range(NC):
        bytes_of(ybuf[c].at[pl.ds(0, 96)], y_ssem.at[c], y_rsem.at[c]).wait_send()
        bytes_of(zsend[c].at[pl.ds(0, NZ - 1)], z_ssem.at[c], z_rsem.at[c]).wait_send()
        bytes_of(xsend[c].at[pl.ds(0, NW - 1)], x_ssem.at[c], x_rsem.at[c]).wait_send()


def body(queries, keys, values, text_queries, text_states, packed_pos, image_of):
    dma = pltpu.SemaphoreType.DMA
    scratch = []
    scratch += [pltpu.VMEM((ROWS, n), BF16) for _, _, n in CHUNKS]
    scratch += [pltpu.VMEM((NZ, 16, n // 2), BF16) for _, _, n in CHUNKS] * 2
    scratch += [pltpu.VMEM((NW, NZ, n), BF16) for _, _, n in CHUNKS] * 2
    scratch += [
        pltpu.VMEM((4, ROWS, FEAT), BF16),
        pltpu.VMEM((2, ROWS, FEAT), BF16),
        pltpu.VMEM((2, ROWS, FEAT), BF16),
        pltpu.VMEM((2, 2, 1, TXT, FEAT), BF16),
        pltpu.VMEM((ROWS, FEAT), F32),
        pltpu.VMEM((NZ, 1, ROWS), I32),
        pltpu.VMEM((NZ, 1, ROWS), I32),
        pltpu.VMEM((1, ROWS), I32),
        pltpu.VMEM((NW, 1, ROWS), I32),
        pltpu.VMEM((2, 1, ROWS), I32),
    ]
    scratch += [dma((NC + 1,))] + [dma((NC,))] * 6 + [dma((4,)), dma((4,)), dma((2,)), dma((2,)), dma((4,)), dma((4,))]
    hbm = pl.BlockSpec(memory_space=pl.ANY)
    vmem = pl.BlockSpec(memory_space=pltpu.VMEM)
    return pl.pallas_call(
        kernel,
        out_shape=jax.ShapeDtypeStruct((ROWS, FEAT), BF16),
        in_specs=[hbm] * 5 + [vmem] * 2,
        out_specs=vmem,
        scratch_shapes=scratch,
        compiler_params=pltpu.CompilerParams(collective_id=0, has_side_effects=True, vmem_limit_bytes=48 * 2**20),
    )(queries, keys, values, text_queries, text_states, packed_pos.reshape(1, ROWS), image_of.reshape(1, ROWS))


def solution(mesh):
    return jax.shard_map(
        body,
        mesh=mesh,
        in_specs=(
            P(("seq", "mp"), None),
            P(("seq", "mp"), None),
            P(("seq", "mp"), None),
            P(("seq", "mp"), None),
            P(None, "seq", None, "mp"),
            P("seq"),
            P("seq"),
        ),
        out_specs=P("seq", "mp"),
        check_vma=False,
    )
```

```python
import functools
import math

import jax
import jax.numpy as jnp
from jax import lax
from jax.experimental import pallas as pl
from jax.experimental.pallas import tpu as pltpu
from jax.sharding import PartitionSpec as P

MESH = pl.DeviceIdType.MESH
HD = 128
ROWS = 128
NZ = 16
NW = 8
NY = 4
FEAT = 1024
HEADS = 8
TXT = 300
TXT_PAD = 304
TXT_ROWS = TXT * 2 * HEADS
PIECE = TXT_ROWS // 4
Q, K, V, T = 0, 1, 2, 3
CHUNKS = (
    (K, 0, 512),
    (K, 512, 512),
    (V, 0, 512),
    (V, 512, 512),
    (T, 0, 512),
    (T, 512, 512),
    (Q, 0, 512),
    (Q, 512, 512),
)
NC = len(CHUNKS)
Y_AHEAD = 2
Z_FIRST = 2
F32 = jnp.float32
BF16 = jnp.bfloat16
I32 = jnp.int32


def iota(shape, dim):
    return lax.broadcasted_iota(I32, shape, dim)


def one_hot(condition):
    return jnp.where(condition, 1.0, 0.0).astype(BF16)


def dot(a, b):
    return jnp.dot(a, b, preferred_element_type=F32)


def dot_t(a, b):
    return lax.dot_general(a, b, (((1,), (1,)), ((), ())), preferred_element_type=F32)


def kernel(q_ref, k_ref, v_ref, t_ref, text_ref, pos_ref, img_ref, o_ref, *scratch):
    scratch = list(scratch)
    take = lambda n: [scratch.pop(0) for _ in range(n)]
    ybuf, zsend, zrecv, xsend, xrecv = (take(NC) for _ in range(5))
    (packed, kv, relay, raw, txt, cross, slot_send, slot_recv, row_send, row_recv, img_near) = take(11)
    (local_sem, y_ssem, y_rsem, z_ssem, z_rsem, x_ssem, x_rsem, n_ssem, n_rsem, t_ssem, t_rsem, s_sems, i_sems) = take(13)
    arrays = (q_ref, k_ref, v_ref, t_ref)

    me = lax.axis_index("seq")
    y = lax.axis_index("mp")
    z, w = me // NW, me % NW
    z_device = lambda other: {"seq": other * NW + w}
    w_device = lambda other: {"seq": z * NW + other}
    after = {"seq": lax.rem(me + 1, NZ * NW)}
    before = {"seq": lax.rem(me + NZ * NW - 1, NZ * NW)}

    def remote(src, dst, send, recv, device):
        return pltpu.make_async_remote_copy(
            src_ref=src, dst_ref=dst, send_sem=send, recv_sem=recv, device_id=device, device_id_type=MESH
        )

    def bytes_of(ref, send, recv):
        return remote(ref, ref, send, recv, after)

    barrier = pltpu.get_barrier_semaphore()
    for i in range(1, NY):
        pl.semaphore_signal(barrier, inc=1, device_id={"mp": lax.rem(y + i, NY)}, device_id_type=MESH)

    def greet_z(i, carry):
        pl.semaphore_signal(barrier, inc=1, device_id=z_device(lax.rem(z + i, NZ)), device_id_type=MESH)
        return carry

    lax.fori_loop(1, NZ, greet_z, 0)

    def greet_w(i, carry):
        pl.semaphore_signal(barrier, inc=1, device_id=w_device(lax.rem(w + i, NW)), device_id_type=MESH)
        return carry

    lax.fori_loop(1, NW, greet_w, 0)
    for device in (after, before):
        pl.semaphore_signal(barrier, inc=1, device_id=device, device_id_type=MESH)

    own = []
    for c, (a, first, columns) in enumerate(CHUNKS):
        start = pl.multiple_of(y * FEAT + first, 128)
        own.append(
            pltpu.make_async_copy(
                arrays[a].at[:, pl.ds(start, columns)], ybuf[c].at[pl.ds(pl.multiple_of(y * 32, 32), 32)], local_sem.at[c]
            )
        )
        own[-1].start()
    own_text = pltpu.make_async_copy(text_ref, raw.at[1], local_sem.at[NC])
    own_text.start()

    pos = pos_ref[...]
    target = lax.shift_right_logical(pos, 7)
    slot = pos & (ROWS - 1)
    image = img_ref[...]
    out_row = iota((2 * ROWS, ROWS), 0)
    same = (lax.shift_right_logical(out_row, 4) * NW + (out_row & 7)) == target
    right_half = (out_row & 8) == 8
    send_plane = one_hot(iota((ROWS, ROWS), 0) == (target & 7) * NZ + lax.shift_right_logical(target, 3))
    send_left = one_hot(same & ~right_half)
    send_right = one_hot(same & right_half)
    to_z = one_hot(iota((NZ, ROWS), 0) == lax.shift_right_logical(target, 3))
    lane_of = (target & 7) * NZ + z
    by_lane = jnp.where(iota((ROWS, ROWS), 0) == lane_of, slot.astype(F32), 0.0).astype(BF16)
    slots = dot_t(to_z, by_lane).astype(I32)
    for i in range(NZ):
        slot_send[i] = slots[i : i + 1]

    with jax.named_scope("greeting"):
        pl.semaphore_wait(barrier, NY - 1 + NZ - 1 + NW - 1 + 2)

    def send_y(c):
        a, first, columns = CHUNKS[c]
        for i in range(1, NY):
            other = lax.rem(y + i, NY)
            start = pl.multiple_of(other * FEAT + first, 128)
            remote(
                arrays[a].at[:, pl.ds(start, columns)],
                ybuf[c].at[pl.ds(pl.multiple_of(y * 32, 32), 32)],
                y_ssem.at[c],
                y_rsem.at[c],
                {"mp": other},
            ).start()

    for c in range(Y_AHEAD):
        send_y(c)

    @pl.when(w < NW - 1)
    def _():
        remote(text_ref, raw.at[0], t_ssem.at[0], t_rsem.at[0], after).start()

    @pl.when(w == NW - 1)
    def _():
        for j in range(3):
            remote(
                text_ref.at[pl.ds(j * PIECE, PIECE)], relay.at[0], t_ssem.at[1], t_rsem.at[1], w_device(2 * j + 1)
            ).start()
        remote(
            text_ref.at[pl.ds(3 * PIECE, PIECE)], relay.at[1], t_ssem.at[2], t_rsem.at[2], z_device(lax.rem(z + 1, NZ))
        ).start()

    def relay_up():
        @pl.when((w % 2 == 1) & (w < NW - 1))
        def _():
            bytes_of(relay.at[0], t_ssem.at[1], t_rsem.at[1]).wait_recv()
            remote(relay.at[0], relay.at[1], t_ssem.at[2], t_rsem.at[2], z_device(lax.rem(z + 1, NZ))).start()

    def relay_in():
        @pl.when(w % 2 == 1)
        def _():
            bytes_of(relay.at[1], t_ssem.at[2], t_rsem.at[2]).wait_recv()
            piece = raw.at[0, pl.ds(pl.multiple_of((w // 2) * PIECE, 16), PIECE)]
            remote(relay.at[1], piece, t_ssem.at[3], t_rsem.at[0], w_device(0)).start()

    def far_first(i):
        return lax.rem(z + 8 + jnp.where(i % 2 == 0, -(i // 2), i // 2), NZ)

    def send_slots(i, carry):
        to = far_first(i)
        remote(slot_send.at[to], slot_recv.at[z], s_sems.at[0], s_sems.at[1], z_device(to)).start()
        return carry

    lax.fori_loop(1, NZ, send_slots, 0)
    slot_recv[z] = slot_send[z]
    remote(img_ref, img_near.at[0], i_sems.at[0], i_sems.at[1], after).start()
    remote(img_ref, img_near.at[1], i_sems.at[2], i_sems.at[3], before).start()

    def after_y(c):
        with jax.named_scope(f"mp_arrival_{c}"):
            own[c].wait()
            bytes_of(ybuf[c].at[pl.ds(0, 96)], y_ssem.at[c], y_rsem.at[c]).wait_recv()
        if c + Y_AHEAD < NC:
            send_y(c + Y_AHEAD)

    def over_z(c, left, right, rows):
        half = CHUNKS[c][2] // 2
        out = dot(left, rows[:, :half]) + dot(right, rows[:, half:])
        zsend[c][...] = out.astype(BF16).reshape(NZ, 16, half)

        def send_z(i, carry):
            to = far_first(i)
            remote(zsend[c].at[to], zrecv[c].at[z], z_ssem.at[c], z_rsem.at[c], z_device(to)).start()
            return carry

        lax.fori_loop(1, NZ, send_z, 0)
        zrecv[c][z] = zsend[c][z]

    def over_plane(c):
        def send_x(i, carry):
            to = lax.rem(w + i, NW)
            remote(xsend[c].at[to], xrecv[c].at[w], x_ssem.at[c], x_rsem.at[c], w_device(to)).start()
            return carry

        lax.fori_loop(1, NW, send_x, 0)
        xrecv[c][w] = xsend[c][w]

    def plane_first(c):
        after_y(c)
        xsend[c][...] = dot(send_plane, ybuf[c][...]).astype(BF16).reshape(NW, NZ, CHUNKS[c][2])
        over_plane(c)

    def from_plane(c):
        with jax.named_scope(f"plane_arrival_{c}"):
            bytes_of(xrecv[c].at[pl.ds(0, NW - 1)], x_ssem.at[c], x_rsem.at[c]).wait_recv()
        return xrecv[c][...].reshape(ROWS, CHUNKS[c][2])

    for c in range(Z_FIRST):
        after_y(c)
        over_z(c, send_left, send_right, ybuf[c][...])
    plane_first(Z_FIRST)
    relay_up()

    by_head_row, by_head_col = iota((256, 256), 0), iota((256, 256), 1)
    by_head = one_hot(
        by_head_col
        == (by_head_row & 15) * 16 + lax.shift_right_logical(by_head_row, 5) * 2 + (lax.shift_right_logical(by_head_row, 4) & 1)
    )

    def sort_prompt(p):
        def two_groups(g, carry):
            first = raw[p, pl.ds(pl.multiple_of(g * 512, 512), 256)]
            second = raw[p, pl.ds(pl.multiple_of(g * 512 + 256, 256), 256)]
            out = dot(by_head, jnp.concatenate([first, second], axis=1)).astype(BF16)
            for i in range(2):
                place_at = pl.ds(pl.multiple_of(g * 32 + 16 * i, 16), 16)
                txt[p, :, :, place_at, :] = out[:, i * HD : (i + 1) * HD].reshape(HEADS, 2, 16, HD)
            return carry

        lax.fori_loop(0, 9, two_groups, 0)
        out = dot(by_head[:, :192], raw[p, 4608:4800]).astype(BF16)
        txt[p, :, :, 288:304, :] = out.reshape(HEADS, 2, 16, HD)

    with jax.named_scope("own_prompt"):
        own_text.wait()
        sort_prompt(1)

    bytes_of(slot_recv.at[pl.ds(0, NZ - 1)], s_sems.at[0], s_sems.at[1]).wait_recv()
    row = slot_recv[0]
    for i in range(1, NZ):
        row = row + slot_recv[i]
    row_send[...] = row

    def send_row(i, carry):
        to = lax.rem(w + i, NW)
        remote(row_send, row_recv.at[w], s_sems.at[2], s_sems.at[3], w_device(to)).start()
        return carry

    lax.fori_loop(1, NW, send_row, 0)
    row_recv[w] = row
    bytes_of(row_recv.at[pl.ds(0, NW - 1)], s_sems.at[2], s_sems.at[3]).wait_recv()
    rows = jnp.concatenate([row_recv[i] for i in range(NW)], axis=0)
    pick = one_hot(iota((ROWS, ROWS), 0) == w * NZ + (iota((ROWS, ROWS), 1) & (NZ - 1)))
    landed = dot(rows.astype(F32).astype(BF16), pick)
    mine = lax.shift_right_logical(iota((NW, ROWS), 1), 4) == iota((NW, ROWS), 0)
    landing = jnp.sum(jnp.where(mine, landed, 0.0), axis=0, keepdims=True).astype(I32)
    place = one_hot(iota((ROWS, ROWS), 0) == landing)

    count = lambda flags: jnp.sum(jnp.where(flags, 1.0, 0.0), axis=1, keepdims=True).astype(I32)
    for i in range(2):
        bytes_of(img_near.at[i], i_sems.at[2 * i], i_sems.at[2 * i + 1]).wait_recv()
    cut = count(image < me)
    cut_prev = count(img_near[0] < me - 1)
    cut_next = count(img_near[1] == me)
    earlier = iota((ROWS, ROWS), 0) < cut
    query_row, key_row = iota((ROWS, 3 * ROWS), 0), iota((ROWS, 3 * ROWS), 1)
    mask = ((query_row < cut) & (key_row >= cut_prev) & (key_row < ROWS + cut)) | (
        (query_row >= cut) & (key_row >= ROWS + cut) & (key_row < 2 * ROWS + cut_next)
    )
    earlier_text = iota((ROWS, TXT_PAD), 0) < cut
    is_text = iota((ROWS, TXT_PAD), 1) < TXT
    scale = math.log2(math.e) / math.sqrt(HD)

    mid_row, mid_col = iota((ROWS, 2 * ROWS), 0), iota((ROWS, 2 * ROWS), 1)
    from_row = (mid_row & (NZ - 1)) * 16 + lax.shift_right_logical(mid_row, 4)
    mid_left = one_hot(mid_col == from_row)
    mid_right = one_hot(mid_col == from_row + 8)
    place_left = dot(place, mid_left).astype(BF16)
    place_right = dot(place, mid_right).astype(BF16)
    row_of, col_of = iota((2 * ROWS, ROWS), 0), iota((2 * ROWS, ROWS), 1)
    to_row = (col_of & (NZ - 1)) * 16 + lax.shift_right_logical(col_of, 4)
    back_left = one_hot(row_of == to_row)
    back_right = one_hot(row_of == to_row + 8)

    def cross_head(h):
        cols = slice(h * HD, (h + 1) * HD)
        query = packed[1, :, cols]
        scores = jnp.where(earlier_text, dot_t(query, txt[0, h, 0]), dot_t(query, txt[1, h, 0]))
        scores = jnp.where(is_text, scores, -1e30)
        top = jnp.max(scores, axis=1, keepdims=True)
        expo = jnp.exp2((scores - top) * scale)
        weights = (expo * (1.0 / jnp.sum(expo, axis=1, keepdims=True))).astype(BF16)
        cross[:, cols] = jnp.where(earlier, dot(weights, txt[0, h, 1]), dot(weights, txt[1, h, 1]))

    ones = jnp.ones((3 * ROWS, HD), BF16)

    def self_head(h):
        cols = slice(h * HD, (h + 1) * HD)
        scores = jnp.where(mask, dot_t(packed[0, :, cols], kv[0, :, cols]), -1e30)
        top = jnp.max(scores, axis=1, keepdims=True)
        weights = jnp.exp2((scores - top) * scale).astype(BF16)
        o_ref[:, cols] = (dot(weights, kv[1, :, cols]) / dot(weights, ones) + cross[:, cols]).astype(BF16)

    near = [c for c, (a, _, _) in enumerate(CHUNKS) if a in (K, V)]

    def near_part(c, side):
        a, first, columns = CHUNKS[c]
        return kv.at[a - K, pl.ds(2 * ROWS * side, ROWS), pl.ds(first, columns)]

    def from_z(c):
        with jax.named_scope(f"z_arrival_{c}"):
            bytes_of(zrecv[c].at[pl.ds(0, NZ - 1)], z_ssem.at[c], z_rsem.at[c]).wait_recv()
        return zrecv[c][...].reshape(2 * ROWS, CHUNKS[c][2] // 2)

    def plane_last(c):
        half = CHUNKS[c][2] // 2
        arrived = from_z(c)
        xsend[c][:, :, :half] = dot(mid_left, arrived).astype(BF16).reshape(NW, NZ, half)
        xsend[c][:, :, half:] = dot(mid_right, arrived).astype(BF16).reshape(NW, NZ, half)
        over_plane(c)

    def use(c, left, right):
        a, first, columns = CHUNKS[c]
        heads = range(first // HD, (first + columns) // HD)
        if a in (K, V):
            kv[a - K, ROWS : 2 * ROWS, first : first + columns // 2] = left
            kv[a - K, ROWS : 2 * ROWS, first + columns // 2 : first + columns] = right
            cols, i = pl.ds(first, columns), near.index(c)
            mine = kv.at[a - K, pl.ds(ROWS, ROWS), cols]
            remote(mine, kv.at[a - K, pl.ds(0, ROWS), cols], n_ssem.at[2 * i], n_rsem.at[2 * i], after).start()
            remote(mine, kv.at[a - K, pl.ds(2 * ROWS, ROWS), cols], n_ssem.at[2 * i + 1], n_rsem.at[2 * i + 1], before).start()
            return
        packed[int(a == T), :, first : first + columns // 2] = left
        packed[int(a == T), :, first + columns // 2 : first + columns] = right
        if a == T:
            if first == 0:
                with jax.named_scope("prompt_arrival"):
                    bytes_of(raw.at[0], t_ssem.at[0], t_rsem.at[0]).wait_recv()
                with jax.named_scope("earlier_prompt"):
                    sort_prompt(0)
            with jax.named_scope("cross_attention"):
                for h in heads:
                    cross_head(h)
            return
        if first == 0:
            with jax.named_scope("near_arrival"):
                for i, n in enumerate(near):
                    for side in range(2):
                        bytes_of(near_part(n, side), n_ssem.at[2 * i + side], n_rsem.at[2 * i + side]).wait_recv()
        with jax.named_scope(f"self_attention_{c}"):
            for h in heads:
                self_head(h)

    def use_from_plane(c):
        rows = from_plane(c)
        half = CHUNKS[c][2] // 2
        use(c, dot(place, rows[:, :half]).astype(BF16), dot(place, rows[:, half:]).astype(BF16))

    for c in range(NC):
        if c < Z_FIRST:
            plane_last(c)
        else:
            arrived = from_z(c)
        if c + Z_FIRST < NC:
            over_z(c + Z_FIRST, back_left, back_right, from_plane(c + Z_FIRST))
        if c + Z_FIRST + 1 < NC:
            plane_first(c + Z_FIRST + 1)
        if c == 1:
            relay_in()
        if 0 < c <= Z_FIRST:
            use_from_plane(c - 1)
        if c >= Z_FIRST:
            use(c, dot(place_left, arrived).astype(BF16), dot(place_right, arrived).astype(BF16))

    @pl.when(w < NW - 1)
    def _():
        bytes_of(raw.at[0], t_ssem.at[0], t_rsem.at[0]).wait_send()

    @pl.when(w == NW - 1)
    def _():
        bytes_of(raw.at[0, pl.ds(0, 3 * PIECE)], t_ssem.at[1], t_rsem.at[1]).wait_send()

    @pl.when(w % 2 == 1)
    def _():
        bytes_of(relay.at[1], t_ssem.at[2], t_rsem.at[2]).wait_send()
        bytes_of(relay.at[1], t_ssem.at[3], t_rsem.at[3]).wait_send()

    bytes_of(slot_send.at[pl.ds(0, NZ - 1)], s_sems.at[0], s_sems.at[1]).wait_send()
    bytes_of(row_recv.at[pl.ds(0, NW - 1)], s_sems.at[2], s_sems.at[3]).wait_send()
    for i in range(2):
        bytes_of(img_near.at[i], i_sems.at[2 * i], i_sems.at[2 * i + 1]).wait_send()
    for i, n in enumerate(near):
        for side in range(2):
            bytes_of(near_part(n, side), n_ssem.at[2 * i + side], n_rsem.at[2 * i + side]).wait_send()
    for c in range(NC):
        bytes_of(ybuf[c].at[pl.ds(0, 96)], y_ssem.at[c], y_rsem.at[c]).wait_send()
        bytes_of(zsend[c].at[pl.ds(0, NZ - 1)], z_ssem.at[c], z_rsem.at[c]).wait_send()
        bytes_of(xsend[c].at[pl.ds(0, NW - 1)], x_ssem.at[c], x_rsem.at[c]).wait_send()


def body(queries, keys, values, text_queries, text_states, packed_pos, image_of):
    dma = pltpu.SemaphoreType.DMA
    scratch = []
    scratch += [pltpu.VMEM((ROWS, n), BF16) for _, _, n in CHUNKS]
    scratch += [pltpu.VMEM((NZ, 16, n // 2), BF16) for _, _, n in CHUNKS] * 2
    scratch += [pltpu.VMEM((NW, NZ, n), BF16) for _, _, n in CHUNKS] * 2
    scratch += [
        pltpu.VMEM((2, ROWS, FEAT), BF16),
        pltpu.VMEM((2, 3 * ROWS, FEAT), BF16),
        pltpu.VMEM((2, PIECE, HD), BF16),
        pltpu.VMEM((2, TXT_ROWS, HD), BF16),
        pltpu.VMEM((2, HEADS, 2, TXT_PAD, HD), BF16),
        pltpu.VMEM((ROWS, FEAT), F32),
        pltpu.VMEM((NZ, 1, ROWS), I32),
        pltpu.VMEM((NZ, 1, ROWS), I32),
        pltpu.VMEM((1, ROWS), I32),
        pltpu.VMEM((NW, 1, ROWS), I32),
        pltpu.VMEM((2, 1, ROWS), I32),
    ]
    scratch += [dma((NC + 1,))] + [dma((NC,))] * 6 + [dma((2 * NC,))] * 2 + [dma((4,))] * 4
    hbm = pl.BlockSpec(memory_space=pl.ANY)
    vmem = pl.BlockSpec(memory_space=pltpu.VMEM)
    prompt = text_states.transpose(1, 2, 0, 3).reshape(TXT, 2, HEADS, HD).transpose(0, 2, 1, 3).reshape(TXT_ROWS, HD)
    return pl.pallas_call(
        kernel,
        out_shape=jax.ShapeDtypeStruct((ROWS, FEAT), BF16),
        in_specs=[hbm] * 5 + [vmem] * 2,
        out_specs=vmem,
        scratch_shapes=scratch,
        compiler_params=pltpu.CompilerParams(collective_id=0, has_side_effects=True, vmem_limit_bytes=60 * 2**20),
    )(queries, keys, values, text_queries, prompt, packed_pos.reshape(1, ROWS), image_of.reshape(1, ROWS))


def solution(mesh):
    return jax.shard_map(
        body,
        mesh=mesh,
        in_specs=(
            P(("seq", "mp"), None),
            P(("seq", "mp"), None),
            P(("seq", "mp"), None),
            P(("seq", "mp"), None),
            P(None, "seq", None, "mp"),
            P("seq"),
            P("seq"),
        ),
        out_specs=P("seq", "mp"),
        check_vma=False,
    )
```

```python
import functools
import math

import jax
import jax.numpy as jnp
from jax import lax
from jax.experimental import pallas as pl
from jax.experimental.pallas import tpu as pltpu
from jax.sharding import PartitionSpec as P

MESH = pl.DeviceIdType.MESH
HD = 128
ROWS = 128
NZ = 16
NW = 8
NY = 4
FEAT = 1024
HEADS = 8
TXT = 300
TXT_PAD = 304
TXT_ROWS = TXT * 2 * HEADS
PIECE = TXT_ROWS // 4
Q, K, V, T = 0, 1, 2, 3
CHUNKS = (
    (K, 0, 512),
    (K, 512, 512),
    (V, 0, 512),
    (V, 512, 512),
    (T, 0, 512),
    (T, 512, 512),
    (Q, 0, 512),
    (Q, 512, 512),
)
NC = len(CHUNKS)
Y_AHEAD = 2
Z_FIRST = 3
F32 = jnp.float32
BF16 = jnp.bfloat16
I32 = jnp.int32


def iota(shape, dim):
    return lax.broadcasted_iota(I32, shape, dim)


def one_hot(condition):
    return jnp.where(condition, 1.0, 0.0).astype(BF16)


def dot(a, b):
    return jnp.dot(a, b, preferred_element_type=F32)


def dot_t(a, b):
    return lax.dot_general(a, b, (((1,), (1,)), ((), ())), preferred_element_type=F32)


def kernel(q_ref, k_ref, v_ref, t_ref, text_ref, pos_ref, img_ref, o_ref, *scratch):
    scratch = list(scratch)
    take = lambda n: [scratch.pop(0) for _ in range(n)]
    ybuf, zsend, zrecv, xsend, xrecv = (take(NC) for _ in range(5))
    (packed, kv, relay, near_relay, raw, txt, cross, slot_send, slot_recv, row_send, row_recv, img_near) = take(12)
    (local_sem, y_ssem, y_rsem, z_ssem, z_rsem, x_ssem, x_rsem, n_ssem, n_rsem, t_ssem, t_rsem, s_sems, i_sems, r_sems) = take(14)
    arrays = (q_ref, k_ref, v_ref, t_ref)

    me = lax.axis_index("seq")
    y = lax.axis_index("mp")
    z, w = me // NW, me % NW
    z_device = lambda other: {"seq": other * NW + w}
    w_device = lambda other: {"seq": z * NW + other}
    after = {"seq": lax.rem(me + 1, NZ * NW)}
    before = {"seq": lax.rem(me + NZ * NW - 1, NZ * NW)}

    def remote(src, dst, send, recv, device):
        return pltpu.make_async_remote_copy(
            src_ref=src, dst_ref=dst, send_sem=send, recv_sem=recv, device_id=device, device_id_type=MESH
        )

    def bytes_of(ref, send, recv):
        return remote(ref, ref, send, recv, after)

    barrier = pltpu.get_barrier_semaphore()
    for i in range(1, NY):
        pl.semaphore_signal(barrier, inc=1, device_id={"mp": lax.rem(y + i, NY)}, device_id_type=MESH)

    def greet_z(i, carry):
        pl.semaphore_signal(barrier, inc=1, device_id=z_device(lax.rem(z + i, NZ)), device_id_type=MESH)
        return carry

    lax.fori_loop(1, NZ, greet_z, 0)

    def greet_w(i, carry):
        pl.semaphore_signal(barrier, inc=1, device_id=w_device(lax.rem(w + i, NW)), device_id_type=MESH)
        return carry

    lax.fori_loop(1, NW, greet_w, 0)
    for device in (after, before):
        pl.semaphore_signal(barrier, inc=1, device_id=device, device_id_type=MESH)

    up = {"seq": lax.rem(z + 1, NZ) * NW}
    down = {"seq": lax.rem(z + NZ - 1, NZ) * NW + NW - 1}

    @pl.when(w == 0)
    def _():
        for i in (1, 3, 5):
            pl.semaphore_signal(
                barrier, inc=1, device_id={"seq": lax.rem(z + NZ - 1, NZ) * NW + i}, device_id_type=MESH
            )

    @pl.when(w == NW - 1)
    def _():
        for i in (2, 4, 6):
            pl.semaphore_signal(barrier, inc=1, device_id={"seq": lax.rem(z + 1, NZ) * NW + i}, device_id_type=MESH)

    inner = (w > 0) & (w < NW - 1)

    own = []
    for c, (a, first, columns) in enumerate(CHUNKS):
        start = pl.multiple_of(y * FEAT + first, 128)
        own.append(
            pltpu.make_async_copy(
                arrays[a].at[:, pl.ds(start, columns)], ybuf[c].at[pl.ds(pl.multiple_of(y * 32, 32), 32)], local_sem.at[c]
            )
        )
        own[-1].start()
    own_text = pltpu.make_async_copy(text_ref, raw.at[1], local_sem.at[NC])
    own_text.start()

    with jax.named_scope("greeting"):
        pl.semaphore_wait(barrier, NY - 1 + NZ - 1 + NW - 1 + 2 + jnp.minimum(w, 1) * jnp.minimum(NW - 1 - w, 1))

    def send_y(c):
        a, first, columns = CHUNKS[c]
        for i in range(1, NY):
            other = lax.rem(y + i, NY)
            start = pl.multiple_of(other * FEAT + first, 128)
            remote(
                arrays[a].at[:, pl.ds(start, columns)],
                ybuf[c].at[pl.ds(pl.multiple_of(y * 32, 32), 32)],
                y_ssem.at[c],
                y_rsem.at[c],
                {"mp": other},
            ).start()

    for c in range(Y_AHEAD):
        send_y(c)

    @pl.when(w < NW - 1)
    def _():
        remote(text_ref, raw.at[0], t_ssem.at[0], t_rsem.at[0], after).start()

    @pl.when(w == NW - 1)
    def _():
        for j in range(3):
            remote(text_ref.at[pl.ds(j * PIECE, PIECE)], relay, t_ssem.at[1], t_rsem.at[1], w_device(2 * j + 1)).start()
        remote(
            text_ref.at[pl.ds(3 * PIECE, PIECE)], raw.at[0, pl.ds(3 * PIECE, PIECE)], t_ssem.at[2], t_rsem.at[0], after
        ).start()

    def relay_prompt():
        @pl.when((w % 2 == 1) & inner)
        def _():
            bytes_of(relay, t_ssem.at[1], t_rsem.at[1]).wait_recv()
            piece = raw.at[0, pl.ds(pl.multiple_of((w // 2) * PIECE, 16), PIECE)]
            remote(relay, piece, t_ssem.at[2], t_rsem.at[0], up).start()

    def relay_near():
        def forward(device, side):
            i = w // 2
            cols = pl.ds(pl.multiple_of((i % 2) * 512, 512), 512)
            bytes_of(near_relay, r_sems.at[0], r_sems.at[1]).wait_recv()
            remote(
                near_relay, kv.at[i // 2, pl.ds(2 * ROWS * side, ROWS), cols], r_sems.at[0], n_rsem.at[2 * i + side], device
            ).start()

        @pl.when((w % 2 == 1) & inner)
        def _():
            forward(up, 0)

        @pl.when((w % 2 == 0) & inner)
        def _():
            forward(down, 1)

    pos = pos_ref[...]
    target = lax.shift_right_logical(pos, 7)
    slot = pos & (ROWS - 1)
    image = img_ref[...]
    out_row = iota((2 * ROWS, ROWS), 0)
    same = (lax.shift_right_logical(out_row, 4) * NW + (out_row & 7)) == target
    right_half = (out_row & 8) == 8
    send_plane = one_hot(iota((ROWS, ROWS), 0) == (target & 7) * NZ + lax.shift_right_logical(target, 3))
    send_left = one_hot(same & ~right_half)
    send_right = one_hot(same & right_half)
    to_z = one_hot(iota((NZ, ROWS), 0) == lax.shift_right_logical(target, 3))
    lane_of = (target & 7) * NZ + z
    by_lane = jnp.where(iota((ROWS, ROWS), 0) == lane_of, slot.astype(F32), 0.0).astype(BF16)
    slots = dot_t(to_z, by_lane).astype(I32)
    for i in range(NZ):
        slot_send[i] = slots[i : i + 1]

    def far_first(i):
        return lax.rem(z + 8 + jnp.where(i % 2 == 0, -(i // 2), i // 2), NZ)

    def send_slots(i, carry):
        to = far_first(i)
        remote(slot_send.at[to], slot_recv.at[z], s_sems.at[0], s_sems.at[1], z_device(to)).start()
        return carry

    lax.fori_loop(1, NZ, send_slots, 0)
    slot_recv[z] = slot_send[z]
    remote(img_ref, img_near.at[0], i_sems.at[0], i_sems.at[1], after).start()
    remote(img_ref, img_near.at[1], i_sems.at[2], i_sems.at[3], before).start()

    def after_y(c):
        with jax.named_scope(f"mp_arrival_{c}"):
            own[c].wait()
            bytes_of(ybuf[c].at[pl.ds(0, 96)], y_ssem.at[c], y_rsem.at[c]).wait_recv()
        if c + Y_AHEAD < NC:
            send_y(c + Y_AHEAD)

    def over_z(c, left, right, rows):
        half = CHUNKS[c][2] // 2
        out = dot(left, rows[:, :half]) + dot(right, rows[:, half:])
        zsend[c][...] = out.astype(BF16).reshape(NZ, 16, half)

        def send_z(i, carry):
            to = far_first(i)
            remote(zsend[c].at[to], zrecv[c].at[z], z_ssem.at[c], z_rsem.at[c], z_device(to)).start()
            return carry

        lax.fori_loop(1, NZ, send_z, 0)
        zrecv[c][z] = zsend[c][z]

    def over_plane(c):
        def send_x(i, carry):
            to = lax.rem(w + i, NW)
            remote(xsend[c].at[to], xrecv[c].at[w], x_ssem.at[c], x_rsem.at[c], w_device(to)).start()
            return carry

        lax.fori_loop(1, NW, send_x, 0)
        xrecv[c][w] = xsend[c][w]

    def plane_first(c):
        after_y(c)
        xsend[c][...] = dot(send_plane, ybuf[c][...]).astype(BF16).reshape(NW, NZ, CHUNKS[c][2])
        over_plane(c)

    def from_plane(c):
        with jax.named_scope(f"plane_arrival_{c}"):
            bytes_of(xrecv[c].at[pl.ds(0, NW - 1)], x_ssem.at[c], x_rsem.at[c]).wait_recv()
        return xrecv[c][...].reshape(ROWS, CHUNKS[c][2])

    for c in range(Z_FIRST):
        after_y(c)
        over_z(c, send_left, send_right, ybuf[c][...])
    plane_first(Z_FIRST)

    by_head_row, by_head_col = iota((256, 256), 0), iota((256, 256), 1)
    by_head = one_hot(
        by_head_col
        == (by_head_row & 15) * 16 + lax.shift_right_logical(by_head_row, 5) * 2 + (lax.shift_right_logical(by_head_row, 4) & 1)
    )

    def sort_prompt(p):
        def two_groups(g, carry):
            first = raw[p, pl.ds(pl.multiple_of(g * 512, 512), 256)]
            second = raw[p, pl.ds(pl.multiple_of(g * 512 + 256, 256), 256)]
            out = dot(by_head, jnp.concatenate([first, second], axis=1)).astype(BF16)
            for i in range(2):
                place_at = pl.ds(pl.multiple_of(g * 32 + 16 * i, 16), 16)
                txt[p, :, :, place_at, :] = out[:, i * HD : (i + 1) * HD].reshape(HEADS, 2, 16, HD)
            return carry

        lax.fori_loop(0, 9, two_groups, 0)
        out = dot(by_head[:, :192], raw[p, 4608:4800]).astype(BF16)
        txt[p, :, :, 288:304, :] = out.reshape(HEADS, 2, 16, HD)

    with jax.named_scope("own_prompt"):
        own_text.wait()
        sort_prompt(1)

    bytes_of(slot_recv.at[pl.ds(0, NZ - 1)], s_sems.at[0], s_sems.at[1]).wait_recv()
    row = slot_recv[0]
    for i in range(1, NZ):
        row = row + slot_recv[i]
    row_send[...] = row

    def send_row(i, carry):
        to = lax.rem(w + i, NW)
        remote(row_send, row_recv.at[w], s_sems.at[2], s_sems.at[3], w_device(to)).start()
        return carry

    lax.fori_loop(1, NW, send_row, 0)
    row_recv[w] = row
    bytes_of(row_recv.at[pl.ds(0, NW - 1)], s_sems.at[2], s_sems.at[3]).wait_recv()
    rows = jnp.concatenate([row_recv[i] for i in range(NW)], axis=0)
    pick = one_hot(iota((ROWS, ROWS), 0) == w * NZ + (iota((ROWS, ROWS), 1) & (NZ - 1)))
    landed = dot(rows.astype(F32).astype(BF16), pick)
    mine = lax.shift_right_logical(iota((NW, ROWS), 1), 4) == iota((NW, ROWS), 0)
    landing = jnp.sum(jnp.where(mine, landed, 0.0), axis=0, keepdims=True).astype(I32)
    place = one_hot(iota((ROWS, ROWS), 0) == landing)

    count = lambda flags: jnp.sum(jnp.where(flags, 1.0, 0.0), axis=1, keepdims=True).astype(I32)
    for i in range(2):
        bytes_of(img_near.at[i], i_sems.at[2 * i], i_sems.at[2 * i + 1]).wait_recv()
    cut = count(image < me)
    cut_prev = count(img_near[0] < me - 1)
    cut_next = count(img_near[1] == me)
    earlier = iota((ROWS, ROWS), 0) < cut
    query_row, key_row = iota((ROWS, 3 * ROWS), 0), iota((ROWS, 3 * ROWS), 1)
    mask = ((query_row < cut) & (key_row >= cut_prev) & (key_row < ROWS + cut)) | (
        (query_row >= cut) & (key_row >= ROWS + cut) & (key_row < 2 * ROWS + cut_next)
    )
    earlier_text = iota((ROWS, TXT_PAD), 0) < cut
    is_text = iota((ROWS, TXT_PAD), 1) < TXT
    scale = math.log2(math.e) / math.sqrt(HD)

    mid_row, mid_col = iota((ROWS, 2 * ROWS), 0), iota((ROWS, 2 * ROWS), 1)
    from_row = (mid_row & (NZ - 1)) * 16 + lax.shift_right_logical(mid_row, 4)
    mid_left = one_hot(mid_col == from_row)
    mid_right = one_hot(mid_col == from_row + 8)
    place_left = dot(place, mid_left).astype(BF16)
    place_right = dot(place, mid_right).astype(BF16)
    row_of, col_of = iota((2 * ROWS, ROWS), 0), iota((2 * ROWS, ROWS), 1)
    to_row = (col_of & (NZ - 1)) * 16 + lax.shift_right_logical(col_of, 4)
    back_left = one_hot(row_of == to_row)
    back_right = one_hot(row_of == to_row + 8)

    def cross_head(h):
        cols = slice(h * HD, (h + 1) * HD)
        query = packed[1, :, cols]
        scores = jnp.where(earlier_text, dot_t(query, txt[0, h, 0]), dot_t(query, txt[1, h, 0]))
        scores = jnp.where(is_text, scores, -1e30)
        top = jnp.max(scores, axis=1, keepdims=True)
        expo = jnp.exp2((scores - top) * scale)
        weights = (expo * (1.0 / jnp.sum(expo, axis=1, keepdims=True))).astype(BF16)
        cross[:, cols] = jnp.where(earlier, dot(weights, txt[0, h, 1]), dot(weights, txt[1, h, 1]))

    ones = jnp.ones((3 * ROWS, HD), BF16)

    def self_head(h):
        cols = slice(h * HD, (h + 1) * HD)
        scores = jnp.where(mask, dot_t(packed[0, :, cols], kv[0, :, cols]), -1e30)
        top = jnp.max(scores, axis=1, keepdims=True)
        weights = jnp.exp2((scores - top) * scale).astype(BF16)
        o_ref[:, cols] = (dot(weights, kv[1, :, cols]) / dot(weights, ones) + cross[:, cols]).astype(BF16)

    near = [c for c, (a, _, _) in enumerate(CHUNKS) if a in (K, V)]

    def near_part(c, side):
        a, first, columns = CHUNKS[c]
        return kv.at[a - K, pl.ds(2 * ROWS * side, ROWS), pl.ds(first, columns)]

    def from_z(c):
        with jax.named_scope(f"z_arrival_{c}"):
            bytes_of(zrecv[c].at[pl.ds(0, NZ - 1)], z_ssem.at[c], z_rsem.at[c]).wait_recv()
        return zrecv[c][...].reshape(2 * ROWS, CHUNKS[c][2] // 2)

    def plane_last(c):
        half = CHUNKS[c][2] // 2
        arrived = from_z(c)
        xsend[c][:, :, :half] = dot(mid_left, arrived).astype(BF16).reshape(NW, NZ, half)
        xsend[c][:, :, half:] = dot(mid_right, arrived).astype(BF16).reshape(NW, NZ, half)
        over_plane(c)

    def use(c, left, right):
        a, first, columns = CHUNKS[c]
        heads = range(first // HD, (first + columns) // HD)
        if a in (K, V):
            kv[a - K, ROWS : 2 * ROWS, first : first + columns // 2] = left
            kv[a - K, ROWS : 2 * ROWS, first + columns // 2 : first + columns] = right
            cols, i = pl.ds(first, columns), near.index(c)
            mine = kv.at[a - K, pl.ds(ROWS, ROWS), cols]
            to_after = (mine, kv.at[a - K, pl.ds(0, ROWS), cols], n_ssem.at[2 * i], n_rsem.at[2 * i], after)
            to_before = (mine, kv.at[a - K, pl.ds(2 * ROWS, ROWS), cols], n_ssem.at[2 * i + 1], n_rsem.at[2 * i + 1], before)

            @pl.when((w < NW - 1) | (i == 3))
            def _():
                remote(*to_after).start()

            @pl.when((w > 0) | (i == 0))
            def _():
                remote(*to_before).start()

            if i < 3:

                @pl.when(w == NW - 1)
                def _():
                    remote(mine, near_relay, n_ssem.at[2 * i], r_sems.at[1], w_device(2 * i + 1)).start()

            if i > 0:

                @pl.when(w == 0)
                def _():
                    remote(mine, near_relay, n_ssem.at[2 * i + 1], r_sems.at[1], w_device(2 * i)).start()

            return
        packed[int(a == T), :, first : first + columns // 2] = left
        packed[int(a == T), :, first + columns // 2 : first + columns] = right
        if a == T:
            if first == 0:
                with jax.named_scope("prompt_arrival"):
                    bytes_of(raw.at[0], t_ssem.at[0], t_rsem.at[0]).wait_recv()
                with jax.named_scope("earlier_prompt"):
                    sort_prompt(0)
            with jax.named_scope("cross_attention"):
                for h in heads:
                    cross_head(h)
            return
        if first == 0:
            with jax.named_scope("near_arrival"):
                for i, n in enumerate(near):
                    for side in range(2):
                        bytes_of(near_part(n, side), n_ssem.at[2 * i + side], n_rsem.at[2 * i + side]).wait_recv()
        with jax.named_scope(f"self_attention_{c}"):
            for h in heads:
                self_head(h)

    def use_from_plane(c):
        rows = from_plane(c)
        half = CHUNKS[c][2] // 2
        use(c, dot(place, rows[:, :half]).astype(BF16), dot(place, rows[:, half:]).astype(BF16))

    for c in range(NC):
        if c < Z_FIRST:
            plane_last(c)
        else:
            arrived = from_z(c)
        if c + Z_FIRST < NC:
            over_z(c + Z_FIRST, back_left, back_right, from_plane(c + Z_FIRST))
        if c + Z_FIRST + 1 < NC:
            plane_first(c + Z_FIRST + 1)
        if c == 1:
            relay_prompt()
        if c == 3:
            relay_near()
        if 0 < c <= Z_FIRST:
            use_from_plane(c - 1)
        if c >= Z_FIRST:
            use(c, dot(place_left, arrived).astype(BF16), dot(place_right, arrived).astype(BF16))

    @pl.when(w < NW - 1)
    def _():
        bytes_of(raw.at[0], t_ssem.at[0], t_rsem.at[0]).wait_send()

    @pl.when(w == NW - 1)
    def _():
        bytes_of(raw.at[0, pl.ds(0, 3 * PIECE)], t_ssem.at[1], t_rsem.at[1]).wait_send()

    @pl.when(w % 2 == 1)
    def _():
        bytes_of(relay, t_ssem.at[2], t_rsem.at[2]).wait_send()

    @pl.when(inner)
    def _():
        bytes_of(near_relay, r_sems.at[0], r_sems.at[1]).wait_send()

    bytes_of(slot_send.at[pl.ds(0, NZ - 1)], s_sems.at[0], s_sems.at[1]).wait_send()
    bytes_of(row_recv.at[pl.ds(0, NW - 1)], s_sems.at[2], s_sems.at[3]).wait_send()
    for i in range(2):
        bytes_of(img_near.at[i], i_sems.at[2 * i], i_sems.at[2 * i + 1]).wait_send()
    for i, n in enumerate(near):
        for side in range(2):
            bytes_of(near_part(n, side), n_ssem.at[2 * i + side], n_rsem.at[2 * i + side]).wait_send()
    for c in range(NC):
        bytes_of(ybuf[c].at[pl.ds(0, 96)], y_ssem.at[c], y_rsem.at[c]).wait_send()
        bytes_of(zsend[c].at[pl.ds(0, NZ - 1)], z_ssem.at[c], z_rsem.at[c]).wait_send()
        bytes_of(xsend[c].at[pl.ds(0, NW - 1)], x_ssem.at[c], x_rsem.at[c]).wait_send()


def body(queries, keys, values, text_queries, text_states, packed_pos, image_of):
    dma = pltpu.SemaphoreType.DMA
    scratch = []
    scratch += [pltpu.VMEM((ROWS, n), BF16) for _, _, n in CHUNKS]
    scratch += [pltpu.VMEM((NZ, 16, n // 2), BF16) for _, _, n in CHUNKS] * 2
    scratch += [pltpu.VMEM((NW, NZ, n), BF16) for _, _, n in CHUNKS] * 2
    scratch += [
        pltpu.VMEM((2, ROWS, FEAT), BF16),
        pltpu.VMEM((2, 3 * ROWS, FEAT), BF16),
        pltpu.VMEM((PIECE, HD), BF16),
        pltpu.VMEM((ROWS, CHUNKS[0][2]), BF16),
        pltpu.VMEM((2, TXT_ROWS, HD), BF16),
        pltpu.VMEM((2, HEADS, 2, TXT_PAD, HD), BF16),
        pltpu.VMEM((ROWS, FEAT), F32),
        pltpu.VMEM((NZ, 1, ROWS), I32),
        pltpu.VMEM((NZ, 1, ROWS), I32),
        pltpu.VMEM((1, ROWS), I32),
        pltpu.VMEM((NW, 1, ROWS), I32),
        pltpu.VMEM((2, 1, ROWS), I32),
    ]
    scratch += [dma((NC + 1,))] + [dma((NC,))] * 6 + [dma((2 * NC,))] * 2 + [dma((4,))] * 4 + [dma((2,))]
    hbm = pl.BlockSpec(memory_space=pl.ANY)
    vmem = pl.BlockSpec(memory_space=pltpu.VMEM)
    prompt = text_states.transpose(1, 2, 0, 3).reshape(TXT, 2, HEADS, HD).transpose(0, 2, 1, 3).reshape(TXT_ROWS, HD)
    return pl.pallas_call(
        kernel,
        out_shape=jax.ShapeDtypeStruct((ROWS, FEAT), BF16),
        in_specs=[hbm] * 5 + [vmem] * 2,
        out_specs=vmem,
        scratch_shapes=scratch,
        compiler_params=pltpu.CompilerParams(collective_id=0, has_side_effects=True, vmem_limit_bytes=60 * 2**20),
    )(queries, keys, values, text_queries, prompt, packed_pos.reshape(1, ROWS), image_of.reshape(1, ROWS))


def solution(mesh):
    return jax.shard_map(
        body,
        mesh=mesh,
        in_specs=(
            P(("seq", "mp"), None),
            P(("seq", "mp"), None),
            P(("seq", "mp"), None),
            P(("seq", "mp"), None),
            P(None, "seq", None, "mp"),
            P("seq"),
            P("seq"),
        ),
        out_specs=P("seq", "mp"),
        check_vma=False,
    )
```

```python
import functools
import math

import jax
import jax.numpy as jnp
from jax import lax
from jax.experimental import pallas as pl
from jax.experimental.pallas import tpu as pltpu
from jax.sharding import PartitionSpec as P

MESH = pl.DeviceIdType.MESH
HD = 128
ROWS = 128
NZ = 16
NW = 8
NY = 4
FEAT = 1024
HEADS = 8
TXT = 300
TXT_PAD = 304
TXT_ROWS = TXT * 2 * HEADS
PIECE = 592
OWN_PIECE = TXT_ROWS - 6 * PIECE
Q, K, V, T = 0, 1, 2, 3
CHUNKS = (
    (K, 0, 512),
    (K, 512, 512),
    (V, 0, 512),
    (V, 512, 512),
    (T, 0, 512),
    (T, 512, 512),
    (Q, 0, 512),
    (Q, 512, 512),
)
NC = len(CHUNKS)
Y_AHEAD = 2
Z_FIRST = 3
F32 = jnp.float32
BF16 = jnp.bfloat16
I32 = jnp.int32


def iota(shape, dim):
    return lax.broadcasted_iota(I32, shape, dim)


def one_hot(condition):
    return jnp.where(condition, 1.0, 0.0).astype(BF16)


def dot(a, b):
    return jnp.dot(a, b, preferred_element_type=F32)


def dot_t(a, b):
    return lax.dot_general(a, b, (((1,), (1,)), ((), ())), preferred_element_type=F32)


def kernel(q_ref, k_ref, v_ref, t_ref, text_ref, pos_ref, img_ref, o_ref, *scratch):
    scratch = list(scratch)
    take = lambda n: [scratch.pop(0) for _ in range(n)]
    ybuf, zsend, zrecv, xsend, xrecv = (take(NC) for _ in range(5))
    (packed, kv, relay, near_relay, raw, txt, cross, slot_send, slot_recv, row_send, row_recv, img_near) = take(12)
    (local_sem, y_ssem, y_rsem, z_ssem, z_rsem, x_ssem, x_rsem, n_ssem, n_rsem, t_ssem, t_rsem, s_sems, i_sems, r_sems) = take(14)
    arrays = (q_ref, k_ref, v_ref, t_ref)

    me = lax.axis_index("seq")
    y = lax.axis_index("mp")
    z, w = me // NW, me % NW
    z_device = lambda other: {"seq": other * NW + w}
    w_device = lambda other: {"seq": z * NW + other}
    after = {"seq": lax.rem(me + 1, NZ * NW)}
    before = {"seq": lax.rem(me + NZ * NW - 1, NZ * NW)}

    def remote(src, dst, send, recv, device):
        return pltpu.make_async_remote_copy(
            src_ref=src, dst_ref=dst, send_sem=send, recv_sem=recv, device_id=device, device_id_type=MESH
        )

    def bytes_of(ref, send, recv):
        return remote(ref, ref, send, recv, after)

    barrier = pltpu.get_barrier_semaphore()
    for i in range(1, NY):
        pl.semaphore_signal(barrier, inc=1, device_id={"mp": lax.rem(y + i, NY)}, device_id_type=MESH)

    def greet_z(i, carry):
        pl.semaphore_signal(barrier, inc=1, device_id=z_device(lax.rem(z + i, NZ)), device_id_type=MESH)
        return carry

    lax.fori_loop(1, NZ, greet_z, 0)

    def greet_w(i, carry):
        pl.semaphore_signal(barrier, inc=1, device_id=w_device(lax.rem(w + i, NW)), device_id_type=MESH)
        return carry

    lax.fori_loop(1, NW, greet_w, 0)
    for device in (after, before):
        pl.semaphore_signal(barrier, inc=1, device_id=device, device_id_type=MESH)

    up = {"seq": lax.rem(z + 1, NZ) * NW}
    down = {"seq": lax.rem(z + NZ - 1, NZ) * NW + NW - 1}

    @pl.when(w == 0)
    def _():
        for i in range(1, NW - 1):
            pl.semaphore_signal(
                barrier, inc=1, device_id={"seq": lax.rem(z + NZ - 1, NZ) * NW + i}, device_id_type=MESH
            )

    @pl.when(w == NW - 1)
    def _():
        for i in (2, 4, 6):
            pl.semaphore_signal(barrier, inc=1, device_id={"seq": lax.rem(z + 1, NZ) * NW + i}, device_id_type=MESH)

    inner = (w > 0) & (w < NW - 1)

    own = []
    for c, (a, first, columns) in enumerate(CHUNKS):
        start = pl.multiple_of(y * FEAT + first, 128)
        own.append(
            pltpu.make_async_copy(
                arrays[a].at[:, pl.ds(start, columns)], ybuf[c].at[pl.ds(pl.multiple_of(y * 32, 32), 32)], local_sem.at[c]
            )
        )
        own[-1].start()
    own_text = pltpu.make_async_copy(text_ref, raw.at[1], local_sem.at[NC])
    own_text.start()

    with jax.named_scope("greeting"):
        pl.semaphore_wait(barrier, NY - 1 + NZ - 1 + NW - 1 + 2 + jnp.minimum(w, 1) * jnp.minimum(NW - 1 - w, 1) * (2 - w % 2))

    def send_y(c):
        a, first, columns = CHUNKS[c]
        for i in range(1, NY):
            other = lax.rem(y + i, NY)
            start = pl.multiple_of(other * FEAT + first, 128)
            remote(
                arrays[a].at[:, pl.ds(start, columns)],
                ybuf[c].at[pl.ds(pl.multiple_of(y * 32, 32), 32)],
                y_ssem.at[c],
                y_rsem.at[c],
                {"mp": other},
            ).start()

    for c in range(Y_AHEAD):
        send_y(c)

    @pl.when(w < NW - 1)
    def _():
        remote(text_ref, raw.at[0], t_ssem.at[0], t_rsem.at[0], after).start()

    @pl.when(w == NW - 1)
    def _():
        for i in range(1, NW - 1):
            remote(text_ref.at[pl.ds((i - 1) * PIECE, PIECE)], relay, t_ssem.at[1], t_rsem.at[1], w_device(i)).start()
        rest = pl.ds(6 * PIECE, OWN_PIECE)
        remote(text_ref.at[rest], raw.at[0, rest], t_ssem.at[2], t_rsem.at[0], after).start()

    def relay_prompt():
        @pl.when(inner)
        def _():
            bytes_of(relay, t_ssem.at[1], t_rsem.at[1]).wait_recv()
            piece = raw.at[0, pl.ds(pl.multiple_of((w - 1) * PIECE, 16), PIECE)]
            remote(relay, piece, t_ssem.at[2], t_rsem.at[0], up).start()

    def relay_near():
        def forward(device, side):
            i = w // 2
            cols = pl.ds(pl.multiple_of((i % 2) * 512, 512), 512)
            bytes_of(near_relay, r_sems.at[0], r_sems.at[1]).wait_recv()
            remote(
                near_relay, kv.at[i // 2, pl.ds(2 * ROWS * side, ROWS), cols], r_sems.at[0], n_rsem.at[2 * i + side], device
            ).start()

        @pl.when((w % 2 == 1) & inner)
        def _():
            forward(up, 0)

        @pl.when((w % 2 == 0) & inner)
        def _():
            forward(down, 1)

    pos = pos_ref[...]
    target = lax.shift_right_logical(pos, 7)
    slot = pos & (ROWS - 1)
    image = img_ref[...]
    out_row = iota((2 * ROWS, ROWS), 0)
    same = (lax.shift_right_logical(out_row, 4) * NW + (out_row & 7)) == target
    right_half = (out_row & 8) == 8
    send_plane = one_hot(iota((ROWS, ROWS), 0) == (target & 7) * NZ + lax.shift_right_logical(target, 3))
    send_left = one_hot(same & ~right_half)
    send_right = one_hot(same & right_half)
    to_z = one_hot(iota((NZ, ROWS), 0) == lax.shift_right_logical(target, 3))
    lane_of = (target & 7) * NZ + z
    by_lane = jnp.where(iota((ROWS, ROWS), 0) == lane_of, slot.astype(F32), 0.0).astype(BF16)
    slots = dot_t(to_z, by_lane).astype(I32)
    for i in range(NZ):
        slot_send[i] = slots[i : i + 1]

    def far_first(i):
        return lax.rem(z + 8 + jnp.where(i % 2 == 0, -(i // 2), i // 2), NZ)

    def send_slots(i, carry):
        to = far_first(i)
        remote(slot_send.at[to], slot_recv.at[z], s_sems.at[0], s_sems.at[1], z_device(to)).start()
        return carry

    lax.fori_loop(1, NZ, send_slots, 0)
    slot_recv[z] = slot_send[z]
    remote(img_ref, img_near.at[0], i_sems.at[0], i_sems.at[1], after).start()
    remote(img_ref, img_near.at[1], i_sems.at[2], i_sems.at[3], before).start()

    def after_y(c):
        with jax.named_scope(f"mp_arrival_{c}"):
            own[c].wait()
            bytes_of(ybuf[c].at[pl.ds(0, 96)], y_ssem.at[c], y_rsem.at[c]).wait_recv()
        if c + Y_AHEAD < NC:
            send_y(c + Y_AHEAD)

    def over_z(c, left, right, rows):
        half = CHUNKS[c][2] // 2
        out = dot(left, rows[:, :half]) + dot(right, rows[:, half:])
        zsend[c][...] = out.astype(BF16).reshape(NZ, 16, half)

        def send_z(i, carry):
            to = far_first(i)
            remote(zsend[c].at[to], zrecv[c].at[z], z_ssem.at[c], z_rsem.at[c], z_device(to)).start()
            return carry

        lax.fori_loop(1, NZ, send_z, 0)
        zrecv[c][z] = zsend[c][z]

    def over_plane(c):
        def send_x(i, carry):
            to = lax.rem(w + i, NW)
            remote(xsend[c].at[to], xrecv[c].at[w], x_ssem.at[c], x_rsem.at[c], w_device(to)).start()
            return carry

        lax.fori_loop(1, NW, send_x, 0)
        xrecv[c][w] = xsend[c][w]

    def plane_first(c):
        after_y(c)
        xsend[c][...] = dot(send_plane, ybuf[c][...]).astype(BF16).reshape(NW, NZ, CHUNKS[c][2])
        over_plane(c)

    def from_plane(c):
        with jax.named_scope(f"plane_arrival_{c}"):
            bytes_of(xrecv[c].at[pl.ds(0, NW - 1)], x_ssem.at[c], x_rsem.at[c]).wait_recv()
        return xrecv[c][...].reshape(ROWS, CHUNKS[c][2])

    for c in range(Z_FIRST):
        after_y(c)
        over_z(c, send_left, send_right, ybuf[c][...])
    plane_first(Z_FIRST)

    by_head_row, by_head_col = iota((256, 256), 0), iota((256, 256), 1)
    by_head = one_hot(
        by_head_col
        == (by_head_row & 15) * 16 + lax.shift_right_logical(by_head_row, 5) * 2 + (lax.shift_right_logical(by_head_row, 4) & 1)
    )

    def sort_prompt(p):
        def two_groups(g, carry):
            first = raw[p, pl.ds(pl.multiple_of(g * 512, 512), 256)]
            second = raw[p, pl.ds(pl.multiple_of(g * 512 + 256, 256), 256)]
            out = dot(by_head, jnp.concatenate([first, second], axis=1)).astype(BF16)
            for i in range(2):
                place_at = pl.ds(pl.multiple_of(g * 32 + 16 * i, 16), 16)
                txt[p, :, :, place_at, :] = out[:, i * HD : (i + 1) * HD].reshape(HEADS, 2, 16, HD)
            return carry

        lax.fori_loop(0, 9, two_groups, 0)
        out = dot(by_head[:, :192], raw[p, 4608:4800]).astype(BF16)
        txt[p, :, :, 288:304, :] = out.reshape(HEADS, 2, 16, HD)

    with jax.named_scope("own_prompt"):
        own_text.wait()
        sort_prompt(1)

    bytes_of(slot_recv.at[pl.ds(0, NZ - 1)], s_sems.at[0], s_sems.at[1]).wait_recv()
    row = slot_recv[0]
    for i in range(1, NZ):
        row = row + slot_recv[i]
    row_send[...] = row

    def send_row(i, carry):
        to = lax.rem(w + i, NW)
        remote(row_send, row_recv.at[w], s_sems.at[2], s_sems.at[3], w_device(to)).start()
        return carry

    lax.fori_loop(1, NW, send_row, 0)
    row_recv[w] = row
    bytes_of(row_recv.at[pl.ds(0, NW - 1)], s_sems.at[2], s_sems.at[3]).wait_recv()
    rows = jnp.concatenate([row_recv[i] for i in range(NW)], axis=0)
    pick = one_hot(iota((ROWS, ROWS), 0) == w * NZ + (iota((ROWS, ROWS), 1) & (NZ - 1)))
    landed = dot(rows.astype(F32).astype(BF16), pick)
    mine = lax.shift_right_logical(iota((NW, ROWS), 1), 4) == iota((NW, ROWS), 0)
    landing = jnp.sum(jnp.where(mine, landed, 0.0), axis=0, keepdims=True).astype(I32)
    place = one_hot(iota((ROWS, ROWS), 0) == landing)

    count = lambda flags: jnp.sum(jnp.where(flags, 1.0, 0.0), axis=1, keepdims=True).astype(I32)
    for i in range(2):
        bytes_of(img_near.at[i], i_sems.at[2 * i], i_sems.at[2 * i + 1]).wait_recv()
    cut = count(image < me)
    cut_prev = count(img_near[0] < me - 1)
    cut_next = count(img_near[1] == me)
    earlier = iota((ROWS, ROWS), 0) < cut
    query_row, key_row = iota((ROWS, 3 * ROWS), 0), iota((ROWS, 3 * ROWS), 1)
    mask = ((query_row < cut) & (key_row >= cut_prev) & (key_row < ROWS + cut)) | (
        (query_row >= cut) & (key_row >= ROWS + cut) & (key_row < 2 * ROWS + cut_next)
    )
    earlier_text = iota((ROWS, TXT_PAD), 0) < cut
    is_text = iota((ROWS, TXT_PAD), 1) < TXT
    scale = math.log2(math.e) / math.sqrt(HD)

    mid_row, mid_col = iota((ROWS, 2 * ROWS), 0), iota((ROWS, 2 * ROWS), 1)
    from_row = (mid_row & (NZ - 1)) * 16 + lax.shift_right_logical(mid_row, 4)
    mid_left = one_hot(mid_col == from_row)
    mid_right = one_hot(mid_col == from_row + 8)
    place_left = dot(place, mid_left).astype(BF16)
    place_right = dot(place, mid_right).astype(BF16)
    row_of, col_of = iota((2 * ROWS, ROWS), 0), iota((2 * ROWS, ROWS), 1)
    to_row = (col_of & (NZ - 1)) * 16 + lax.shift_right_logical(col_of, 4)
    back_left = one_hot(row_of == to_row)
    back_right = one_hot(row_of == to_row + 8)

    def cross_head(h):
        cols = slice(h * HD, (h + 1) * HD)
        query = packed[1, :, cols]
        scores = jnp.where(earlier_text, dot_t(query, txt[0, h, 0]), dot_t(query, txt[1, h, 0]))
        scores = jnp.where(is_text, scores, -1e30)
        top = jnp.max(scores, axis=1, keepdims=True)
        expo = jnp.exp2((scores - top) * scale)
        weights = (expo * (1.0 / jnp.sum(expo, axis=1, keepdims=True))).astype(BF16)
        cross[:, cols] = jnp.where(earlier, dot(weights, txt[0, h, 1]), dot(weights, txt[1, h, 1]))

    ones = jnp.ones((3 * ROWS, HD), BF16)

    def self_head(h):
        cols = slice(h * HD, (h + 1) * HD)
        scores = jnp.where(mask, dot_t(packed[0, :, cols], kv[0, :, cols]), -1e30)
        top = jnp.max(scores, axis=1, keepdims=True)
        weights = jnp.exp2((scores - top) * scale).astype(BF16)
        o_ref[:, cols] = (dot(weights, kv[1, :, cols]) / dot(weights, ones) + cross[:, cols]).astype(BF16)

    near = [c for c, (a, _, _) in enumerate(CHUNKS) if a in (K, V)]

    def near_part(c, side):
        a, first, columns = CHUNKS[c]
        return kv.at[a - K, pl.ds(2 * ROWS * side, ROWS), pl.ds(first, columns)]

    def from_z(c):
        with jax.named_scope(f"z_arrival_{c}"):
            bytes_of(zrecv[c].at[pl.ds(0, NZ - 1)], z_ssem.at[c], z_rsem.at[c]).wait_recv()
        return zrecv[c][...].reshape(2 * ROWS, CHUNKS[c][2] // 2)

    def plane_last(c):
        half = CHUNKS[c][2] // 2
        arrived = from_z(c)
        xsend[c][:, :, :half] = dot(mid_left, arrived).astype(BF16).reshape(NW, NZ, half)
        xsend[c][:, :, half:] = dot(mid_right, arrived).astype(BF16).reshape(NW, NZ, half)
        over_plane(c)

    def use(c, left, right):
        a, first, columns = CHUNKS[c]
        heads = range(first // HD, (first + columns) // HD)
        if a in (K, V):
            kv[a - K, ROWS : 2 * ROWS, first : first + columns // 2] = left
            kv[a - K, ROWS : 2 * ROWS, first + columns // 2 : first + columns] = right
            cols, i = pl.ds(first, columns), near.index(c)
            mine = kv.at[a - K, pl.ds(ROWS, ROWS), cols]
            to_after = (mine, kv.at[a - K, pl.ds(0, ROWS), cols], n_ssem.at[2 * i], n_rsem.at[2 * i], after)
            to_before = (mine, kv.at[a - K, pl.ds(2 * ROWS, ROWS), cols], n_ssem.at[2 * i + 1], n_rsem.at[2 * i + 1], before)

            @pl.when((w < NW - 1) | (i == 3))
            def _():
                remote(*to_after).start()

            @pl.when((w > 0) | (i == 0))
            def _():
                remote(*to_before).start()

            if i < 3:

                @pl.when(w == NW - 1)
                def _():
                    remote(mine, near_relay, n_ssem.at[2 * i], r_sems.at[1], w_device(2 * i + 1)).start()

            if i > 0:

                @pl.when(w == 0)
                def _():
                    remote(mine, near_relay, n_ssem.at[2 * i + 1], r_sems.at[1], w_device(2 * i)).start()

            return
        packed[int(a == T), :, first : first + columns // 2] = left
        packed[int(a == T), :, first + columns // 2 : first + columns] = right
        if a == T:
            return
        if first == 0:
            with jax.named_scope("near_arrival"):
                for i, n in enumerate(near):
                    for side in range(2):
                        bytes_of(near_part(n, side), n_ssem.at[2 * i + side], n_rsem.at[2 * i + side]).wait_recv()
        with jax.named_scope(f"self_attention_{c}"):
            for h in heads:
                self_head(h)

    def use_from_plane(c):
        rows = from_plane(c)
        half = CHUNKS[c][2] // 2
        use(c, dot(place, rows[:, :half]).astype(BF16), dot(place, rows[:, half:]).astype(BF16))

    for c in range(NC):
        if c < Z_FIRST:
            plane_last(c)
        else:
            arrived = from_z(c)
        if c + Z_FIRST < NC:
            over_z(c + Z_FIRST, back_left, back_right, from_plane(c + Z_FIRST))
        if c + Z_FIRST + 1 < NC:
            plane_first(c + Z_FIRST + 1)
        if c == 0:
            relay_prompt()
        if c == 3:
            relay_near()
        if 0 < c <= Z_FIRST:
            use_from_plane(c - 1)
        if c == 5:
            bytes_of(raw.at[0], t_ssem.at[0], t_rsem.at[0]).wait_recv()
            sort_prompt(0)
        if c >= Z_FIRST:
            use(c, dot(place_left, arrived).astype(BF16), dot(place_right, arrived).astype(BF16))
        if c == 5:
            for h in range(HEADS):
                cross_head(h)

    @pl.when(w < NW - 1)
    def _():
        bytes_of(raw.at[0], t_ssem.at[0], t_rsem.at[0]).wait_send()

    @pl.when(w == NW - 1)
    def _():
        bytes_of(raw.at[0, pl.ds(0, 6 * PIECE)], t_ssem.at[1], t_rsem.at[1]).wait_send()
        bytes_of(raw.at[0, pl.ds(0, OWN_PIECE)], t_ssem.at[2], t_rsem.at[2]).wait_send()

    @pl.when(inner)
    def _():
        bytes_of(relay, t_ssem.at[2], t_rsem.at[2]).wait_send()
        bytes_of(near_relay, r_sems.at[0], r_sems.at[1]).wait_send()

    bytes_of(slot_send.at[pl.ds(0, NZ - 1)], s_sems.at[0], s_sems.at[1]).wait_send()
    bytes_of(row_recv.at[pl.ds(0, NW - 1)], s_sems.at[2], s_sems.at[3]).wait_send()
    for i in range(2):
        bytes_of(img_near.at[i], i_sems.at[2 * i], i_sems.at[2 * i + 1]).wait_send()
    for i, n in enumerate(near):
        for side in range(2):
            bytes_of(near_part(n, side), n_ssem.at[2 * i + side], n_rsem.at[2 * i + side]).wait_send()
    for c in range(NC):
        bytes_of(ybuf[c].at[pl.ds(0, 96)], y_ssem.at[c], y_rsem.at[c]).wait_send()
        bytes_of(zsend[c].at[pl.ds(0, NZ - 1)], z_ssem.at[c], z_rsem.at[c]).wait_send()
        bytes_of(xsend[c].at[pl.ds(0, NW - 1)], x_ssem.at[c], x_rsem.at[c]).wait_send()


def body(queries, keys, values, text_queries, text_states, packed_pos, image_of):
    dma = pltpu.SemaphoreType.DMA
    scratch = []
    scratch += [pltpu.VMEM((ROWS, n), BF16) for _, _, n in CHUNKS]
    scratch += [pltpu.VMEM((NZ, 16, n // 2), BF16) for _, _, n in CHUNKS] * 2
    scratch += [pltpu.VMEM((NW, NZ, n), BF16) for _, _, n in CHUNKS] * 2
    scratch += [
        pltpu.VMEM((2, ROWS, FEAT), BF16),
        pltpu.VMEM((2, 3 * ROWS, FEAT), BF16),
        pltpu.VMEM((PIECE, HD), BF16),
        pltpu.VMEM((ROWS, CHUNKS[0][2]), BF16),
        pltpu.VMEM((2, TXT_ROWS, HD), BF16),
        pltpu.VMEM((2, HEADS, 2, TXT_PAD, HD), BF16),
        pltpu.VMEM((ROWS, FEAT), F32),
        pltpu.VMEM((NZ, 1, ROWS), I32),
        pltpu.VMEM((NZ, 1, ROWS), I32),
        pltpu.VMEM((1, ROWS), I32),
        pltpu.VMEM((NW, 1, ROWS), I32),
        pltpu.VMEM((2, 1, ROWS), I32),
    ]
    scratch += [dma((NC + 1,))] + [dma((NC,))] * 6 + [dma((2 * NC,))] * 2 + [dma((4,))] * 4 + [dma((2,))]
    hbm = pl.BlockSpec(memory_space=pl.ANY)
    vmem = pl.BlockSpec(memory_space=pltpu.VMEM)
    prompt = text_states.transpose(1, 2, 0, 3).reshape(TXT, 2, HEADS, HD).transpose(0, 2, 1, 3).reshape(TXT_ROWS, HD)
    return pl.pallas_call(
        kernel,
        out_shape=jax.ShapeDtypeStruct((ROWS, FEAT), BF16),
        in_specs=[hbm] * 5 + [vmem] * 2,
        out_specs=vmem,
        scratch_shapes=scratch,
        compiler_params=pltpu.CompilerParams(collective_id=0, has_side_effects=True, vmem_limit_bytes=60 * 2**20),
    )(queries, keys, values, text_queries, prompt, packed_pos.reshape(1, ROWS), image_of.reshape(1, ROWS))


def solution(mesh):
    return jax.shard_map(
        body,
        mesh=mesh,
        in_specs=(
            P(("seq", "mp"), None),
            P(("seq", "mp"), None),
            P(("seq", "mp"), None),
            P(("seq", "mp"), None),
            P(None, "seq", None, "mp"),
            P("seq"),
            P("seq"),
        ),
        out_specs=P("seq", "mp"),
        check_vma=False,
    )
```

```python
import functools
import math

import jax
import jax.numpy as jnp
from jax import lax
from jax.experimental import pallas as pl
from jax.experimental.pallas import tpu as pltpu
from jax.sharding import PartitionSpec as P

MESH = pl.DeviceIdType.MESH
HD = 128
ROWS = 128
NZ = 16
NW = 8
NY = 4
FEAT = 1024
HEADS = 8
TXT = 300
TXT_PAD = 304
TXT_ROWS = TXT * 2 * HEADS
PIECE = 592
OWN_PIECE = TXT_ROWS - 6 * PIECE
Q, K, V, T = 0, 1, 2, 3
CHUNKS = (
    (K, 0, 512),
    (K, 512, 512),
    (V, 0, 512),
    (V, 512, 512),
    (T, 0, 512),
    (T, 512, 512),
    (Q, 0, 512),
    (Q, 512, 512),
)
NC = len(CHUNKS)
Y_AHEAD = 2
Z_FIRST = 3
F32 = jnp.float32
BF16 = jnp.bfloat16
I32 = jnp.int32


def iota(shape, dim):
    return lax.broadcasted_iota(I32, shape, dim)


def one_hot(condition):
    return jnp.where(condition, 1.0, 0.0).astype(BF16)


def dot(a, b):
    return jnp.dot(a, b, preferred_element_type=F32)


def dot_t(a, b):
    return lax.dot_general(a, b, (((1,), (1,)), ((), ())), preferred_element_type=F32)


def kernel(q_ref, k_ref, v_ref, t_ref, text_ref, pos_ref, img_ref, o_ref, *scratch):
    scratch = list(scratch)
    take = lambda n: [scratch.pop(0) for _ in range(n)]
    ybuf, zsend, zrecv, xsend, xrecv = (take(NC) for _ in range(5))
    (packed, kv, relay, near_relay, raw, txt, cross, slot_send, slot_recv, row_send, row_recv, img_near) = take(12)
    (local_sem, y_ssem, y_rsem, z_ssem, z_rsem, x_ssem, x_rsem, n_ssem, n_rsem, t_ssem, t_rsem, s_sems, i_sems, r_sems) = take(14)
    arrays = (q_ref, k_ref, v_ref, t_ref)

    me = lax.axis_index("seq")
    y = lax.axis_index("mp")
    z, w = me // NW, me % NW
    z_device = lambda other: {"seq": other * NW + w}
    w_device = lambda other: {"seq": z * NW + other}
    after = {"seq": lax.rem(me + 1, NZ * NW)}
    before = {"seq": lax.rem(me + NZ * NW - 1, NZ * NW)}

    def remote(src, dst, send, recv, device):
        return pltpu.make_async_remote_copy(
            src_ref=src, dst_ref=dst, send_sem=send, recv_sem=recv, device_id=device, device_id_type=MESH
        )

    def bytes_of(ref, send, recv):
        return remote(ref, ref, send, recv, after)

    barrier = pltpu.get_barrier_semaphore()
    for i in range(1, NY):
        pl.semaphore_signal(barrier, inc=1, device_id={"mp": lax.rem(y + i, NY)}, device_id_type=MESH)

    def greet_z(i, carry):
        pl.semaphore_signal(barrier, inc=1, device_id=z_device(lax.rem(z + i, NZ)), device_id_type=MESH)
        return carry

    lax.fori_loop(1, NZ, greet_z, 0)

    def greet_w(i, carry):
        pl.semaphore_signal(barrier, inc=1, device_id=w_device(lax.rem(w + i, NW)), device_id_type=MESH)
        return carry

    lax.fori_loop(1, NW, greet_w, 0)
    for device in (after, before):
        pl.semaphore_signal(barrier, inc=1, device_id=device, device_id_type=MESH)

    up = {"seq": lax.rem(z + 1, NZ) * NW}
    down = {"seq": lax.rem(z + NZ - 1, NZ) * NW + NW - 1}

    @pl.when(w == 0)
    def _():
        for i in range(1, NW - 1):
            pl.semaphore_signal(
                barrier, inc=1, device_id={"seq": lax.rem(z + NZ - 1, NZ) * NW + i}, device_id_type=MESH
            )

    @pl.when(w == NW - 1)
    def _():
        for i in (2, 4, 6):
            pl.semaphore_signal(barrier, inc=1, device_id={"seq": lax.rem(z + 1, NZ) * NW + i}, device_id_type=MESH)

    inner = (w > 0) & (w < NW - 1)

    own = []
    for c, (a, first, columns) in enumerate(CHUNKS):
        start = pl.multiple_of(y * FEAT + first, 128)
        own.append(
            pltpu.make_async_copy(
                arrays[a].at[:, pl.ds(start, columns)], ybuf[c].at[pl.ds(pl.multiple_of(y * 32, 32), 32)], local_sem.at[c]
            )
        )
        own[-1].start()
    own_text = pltpu.make_async_copy(text_ref, raw.at[1], local_sem.at[NC])
    own_text.start()

    with jax.named_scope("greeting"):
        pl.semaphore_wait(barrier, NY - 1 + NZ - 1 + NW - 1 + 2 + jnp.minimum(w, 1) * jnp.minimum(NW - 1 - w, 1) * (2 - w % 2))

    def send_y(c):
        a, first, columns = CHUNKS[c]
        for i in range(1, NY):
            other = lax.rem(y + i, NY)
            start = pl.multiple_of(other * FEAT + first, 128)
            remote(
                arrays[a].at[:, pl.ds(start, columns)],
                ybuf[c].at[pl.ds(pl.multiple_of(y * 32, 32), 32)],
                y_ssem.at[c],
                y_rsem.at[c],
                {"mp": other},
            ).start()

    for c in range(Y_AHEAD):
        send_y(c)

    @pl.when(w < NW - 1)
    def _():
        remote(text_ref, raw.at[0], t_ssem.at[0], t_rsem.at[0], after).start()

    @pl.when(w == NW - 1)
    def _():
        for i in range(1, NW - 1):
            remote(text_ref.at[pl.ds((i - 1) * PIECE, PIECE)], relay, t_ssem.at[1], t_rsem.at[1], w_device(i)).start()
        rest = pl.ds(6 * PIECE, OWN_PIECE)
        remote(text_ref.at[rest], raw.at[0, rest], t_ssem.at[2], t_rsem.at[0], after).start()

    def relay_prompt():
        @pl.when(inner)
        def _():
            bytes_of(relay, t_ssem.at[1], t_rsem.at[1]).wait_recv()
            piece = raw.at[0, pl.ds(pl.multiple_of((w - 1) * PIECE, 16), PIECE)]
            remote(relay, piece, t_ssem.at[2], t_rsem.at[0], up).start()

    def relay_near(first, last):
        def forward(device, side):
            i = w // 2
            cols = pl.ds(pl.multiple_of((i % 2) * 512, 512), 512)
            bytes_of(near_relay, r_sems.at[0], r_sems.at[1]).wait_recv()
            remote(
                near_relay, kv.at[i // 2, pl.ds(2 * ROWS * side, ROWS), cols], r_sems.at[0], n_rsem.at[2 * i + side], device
            ).start()

        @pl.when((w % 2 == 1) & (w >= first) & (w <= last))
        def _():
            forward(up, 0)

        @pl.when((w % 2 == 0) & (w >= first) & (w <= last))
        def _():
            forward(down, 1)

    pos = pos_ref[...]
    target = lax.shift_right_logical(pos, 7)
    slot = pos & (ROWS - 1)
    image = img_ref[...]
    out_row = iota((2 * ROWS, ROWS), 0)
    same = (lax.shift_right_logical(out_row, 4) * NW + (out_row & 7)) == target
    right_half = (out_row & 8) == 8
    send_plane = one_hot(iota((ROWS, ROWS), 0) == (target & 7) * NZ + lax.shift_right_logical(target, 3))
    send_left = one_hot(same & ~right_half)
    send_right = one_hot(same & right_half)
    to_z = one_hot(iota((NZ, ROWS), 0) == lax.shift_right_logical(target, 3))
    lane_of = (target & 7) * NZ + z
    by_lane = jnp.where(iota((ROWS, ROWS), 0) == lane_of, slot.astype(F32), 0.0).astype(BF16)
    slots = dot_t(to_z, by_lane).astype(I32)
    for i in range(NZ):
        slot_send[i] = slots[i : i + 1]

    def far_first(i):
        return lax.rem(z + 8 + jnp.where(i % 2 == 0, -(i // 2), i // 2), NZ)

    def send_slots(i, carry):
        to = far_first(i)
        remote(slot_send.at[to], slot_recv.at[z], s_sems.at[0], s_sems.at[1], z_device(to)).start()
        return carry

    lax.fori_loop(1, NZ, send_slots, 0)
    slot_recv[z] = slot_send[z]
    remote(img_ref, img_near.at[0], i_sems.at[0], i_sems.at[1], after).start()
    remote(img_ref, img_near.at[1], i_sems.at[2], i_sems.at[3], before).start()

    def after_y(c):
        with jax.named_scope(f"mp_arrival_{c}"):
            own[c].wait()
            bytes_of(ybuf[c].at[pl.ds(0, 96)], y_ssem.at[c], y_rsem.at[c]).wait_recv()
        if c + Y_AHEAD < NC:
            send_y(c + Y_AHEAD)

    def over_z(c, left, right, rows):
        half = CHUNKS[c][2] // 2
        out = dot(left, rows[:, :half]) + dot(right, rows[:, half:])
        zsend[c][...] = out.astype(BF16).reshape(NZ, 16, half)

        def send_z(i, carry):
            to = far_first(i)
            remote(zsend[c].at[to], zrecv[c].at[z], z_ssem.at[c], z_rsem.at[c], z_device(to)).start()
            return carry

        lax.fori_loop(1, NZ, send_z, 0)
        zrecv[c][z] = zsend[c][z]

    def over_plane(c):
        def send_x(i, carry):
            to = lax.rem(w + i, NW)
            remote(xsend[c].at[to], xrecv[c].at[w], x_ssem.at[c], x_rsem.at[c], w_device(to)).start()
            return carry

        lax.fori_loop(1, NW, send_x, 0)
        xrecv[c][w] = xsend[c][w]

    def plane_first(c):
        after_y(c)
        xsend[c][...] = dot(send_plane, ybuf[c][...]).astype(BF16).reshape(NW, NZ, CHUNKS[c][2])
        over_plane(c)

    def from_plane(c):
        with jax.named_scope(f"plane_arrival_{c}"):
            bytes_of(xrecv[c].at[pl.ds(0, NW - 1)], x_ssem.at[c], x_rsem.at[c]).wait_recv()
        return xrecv[c][...].reshape(ROWS, CHUNKS[c][2])

    for c in range(Z_FIRST):
        after_y(c)
        over_z(c, send_left, send_right, ybuf[c][...])
    plane_first(Z_FIRST)

    by_head_row, by_head_col = iota((256, 256), 0), iota((256, 256), 1)
    by_head = one_hot(
        by_head_col
        == (by_head_row & 15) * 16 + lax.shift_right_logical(by_head_row, 5) * 2 + (lax.shift_right_logical(by_head_row, 4) & 1)
    )

    def sort_prompt(p):
        def two_groups(g, carry):
            first = raw[p, pl.ds(pl.multiple_of(g * 512, 512), 256)]
            second = raw[p, pl.ds(pl.multiple_of(g * 512 + 256, 256), 256)]
            out = dot(by_head, jnp.concatenate([first, second], axis=1)).astype(BF16)
            for i in range(2):
                place_at = pl.ds(pl.multiple_of(g * 32 + 16 * i, 16), 16)
                txt[p, :, :, place_at, :] = out[:, i * HD : (i + 1) * HD].reshape(HEADS, 2, 16, HD)
            return carry

        lax.fori_loop(0, 9, two_groups, 0)
        out = dot(by_head[:, :192], raw[p, 4608:4800]).astype(BF16)
        txt[p, :, :, 288:304, :] = out.reshape(HEADS, 2, 16, HD)

    with jax.named_scope("own_prompt"):
        own_text.wait()
        sort_prompt(1)

    bytes_of(slot_recv.at[pl.ds(0, NZ - 1)], s_sems.at[0], s_sems.at[1]).wait_recv()
    row = slot_recv[0]
    for i in range(1, NZ):
        row = row + slot_recv[i]
    row_send[...] = row

    def send_row(i, carry):
        to = lax.rem(w + i, NW)
        remote(row_send, row_recv.at[w], s_sems.at[2], s_sems.at[3], w_device(to)).start()
        return carry

    lax.fori_loop(1, NW, send_row, 0)
    row_recv[w] = row
    bytes_of(row_recv.at[pl.ds(0, NW - 1)], s_sems.at[2], s_sems.at[3]).wait_recv()
    rows = jnp.concatenate([row_recv[i] for i in range(NW)], axis=0)
    pick = one_hot(iota((ROWS, ROWS), 0) == w * NZ + (iota((ROWS, ROWS), 1) & (NZ - 1)))
    landed = dot(rows.astype(F32).astype(BF16), pick)
    mine = lax.shift_right_logical(iota((NW, ROWS), 1), 4) == iota((NW, ROWS), 0)
    landing = jnp.sum(jnp.where(mine, landed, 0.0), axis=0, keepdims=True).astype(I32)
    place = one_hot(iota((ROWS, ROWS), 0) == landing)

    count = lambda flags: jnp.sum(jnp.where(flags, 1.0, 0.0), axis=1, keepdims=True).astype(I32)
    for i in range(2):
        bytes_of(img_near.at[i], i_sems.at[2 * i], i_sems.at[2 * i + 1]).wait_recv()
    cut = count(image < me)
    cut_prev = count(img_near[0] < me - 1)
    cut_next = count(img_near[1] == me)
    earlier = iota((ROWS, ROWS), 0) < cut
    query_row, key_row = iota((ROWS, 3 * ROWS), 0), iota((ROWS, 3 * ROWS), 1)
    mask = ((query_row < cut) & (key_row >= cut_prev) & (key_row < ROWS + cut)) | (
        (query_row >= cut) & (key_row >= ROWS + cut) & (key_row < 2 * ROWS + cut_next)
    )
    earlier_text = iota((ROWS, TXT_PAD), 0) < cut
    is_text = iota((ROWS, TXT_PAD), 1) < TXT
    scale = math.log2(math.e) / math.sqrt(HD)

    mid_row, mid_col = iota((ROWS, 2 * ROWS), 0), iota((ROWS, 2 * ROWS), 1)
    from_row = (mid_row & (NZ - 1)) * 16 + lax.shift_right_logical(mid_row, 4)
    mid_left = one_hot(mid_col == from_row)
    mid_right = one_hot(mid_col == from_row + 8)
    place_left = dot(place, mid_left).astype(BF16)
    place_right = dot(place, mid_right).astype(BF16)
    row_of, col_of = iota((2 * ROWS, ROWS), 0), iota((2 * ROWS, ROWS), 1)
    to_row = (col_of & (NZ - 1)) * 16 + lax.shift_right_logical(col_of, 4)
    back_left = one_hot(row_of == to_row)
    back_right = one_hot(row_of == to_row + 8)

    def cross_head(h):
        cols = slice(h * HD, (h + 1) * HD)
        query = packed[1, :, cols]
        scores = jnp.where(earlier_text, dot_t(query, txt[0, h, 0]), dot_t(query, txt[1, h, 0]))
        scores = jnp.where(is_text, scores, -1e30)
        top = jnp.max(scores, axis=1, keepdims=True)
        expo = jnp.exp2((scores - top) * scale)
        weights = (expo * (1.0 / jnp.sum(expo, axis=1, keepdims=True))).astype(BF16)
        cross[:, cols] = jnp.where(earlier, dot(weights, txt[0, h, 1]), dot(weights, txt[1, h, 1]))

    ones = jnp.ones((3 * ROWS, HD), BF16)

    def self_head(h):
        cols = slice(h * HD, (h + 1) * HD)
        scores = jnp.where(mask, dot_t(packed[0, :, cols], kv[0, :, cols]), -1e30)
        top = jnp.max(scores, axis=1, keepdims=True)
        weights = jnp.exp2((scores - top) * scale).astype(BF16)
        o_ref[:, cols] = (dot(weights, kv[1, :, cols]) / dot(weights, ones) + cross[:, cols]).astype(BF16)

    near = [c for c, (a, _, _) in enumerate(CHUNKS) if a in (K, V)]

    def near_part(c, side):
        a, first, columns = CHUNKS[c]
        return kv.at[a - K, pl.ds(2 * ROWS * side, ROWS), pl.ds(first, columns)]

    def from_z(c):
        with jax.named_scope(f"z_arrival_{c}"):
            bytes_of(zrecv[c].at[pl.ds(0, NZ - 1)], z_ssem.at[c], z_rsem.at[c]).wait_recv()
        return zrecv[c][...].reshape(2 * ROWS, CHUNKS[c][2] // 2)

    def plane_last(c):
        half = CHUNKS[c][2] // 2
        arrived = from_z(c)
        xsend[c][:, :, :half] = dot(mid_left, arrived).astype(BF16).reshape(NW, NZ, half)
        xsend[c][:, :, half:] = dot(mid_right, arrived).astype(BF16).reshape(NW, NZ, half)
        over_plane(c)

    def use(c, left, right):
        a, first, columns = CHUNKS[c]
        heads = range(first // HD, (first + columns) // HD)
        if a in (K, V):
            kv[a - K, ROWS : 2 * ROWS, first : first + columns // 2] = left
            kv[a - K, ROWS : 2 * ROWS, first + columns // 2 : first + columns] = right
            cols, i = pl.ds(first, columns), near.index(c)
            mine = kv.at[a - K, pl.ds(ROWS, ROWS), cols]
            to_after = (mine, kv.at[a - K, pl.ds(0, ROWS), cols], n_ssem.at[2 * i], n_rsem.at[2 * i], after)
            to_before = (mine, kv.at[a - K, pl.ds(2 * ROWS, ROWS), cols], n_ssem.at[2 * i + 1], n_rsem.at[2 * i + 1], before)

            @pl.when((w < NW - 1) | (i == 3))
            def _():
                remote(*to_after).start()

            @pl.when((w > 0) | (i == 0))
            def _():
                remote(*to_before).start()

            if i < 3:

                @pl.when(w == NW - 1)
                def _():
                    remote(mine, near_relay, n_ssem.at[2 * i], r_sems.at[1], w_device(2 * i + 1)).start()

            if i > 0:

                @pl.when(w == 0)
                def _():
                    remote(mine, near_relay, n_ssem.at[2 * i + 1], r_sems.at[1], w_device(2 * i)).start()

            return
        packed[int(a == T), :, first : first + columns // 2] = left
        packed[int(a == T), :, first + columns // 2 : first + columns] = right
        if a == T:
            return
        if first == 0:
            with jax.named_scope("near_arrival"):
                for i, n in enumerate(near):
                    for side in range(2):
                        bytes_of(near_part(n, side), n_ssem.at[2 * i + side], n_rsem.at[2 * i + side]).wait_recv()
        with jax.named_scope(f"self_attention_{c}"):
            for h in heads:
                self_head(h)

    def use_from_plane(c):
        rows = from_plane(c)
        half = CHUNKS[c][2] // 2
        use(c, dot(place, rows[:, :half]).astype(BF16), dot(place, rows[:, half:]).astype(BF16))

    for c in range(NC):
        if c < Z_FIRST:
            plane_last(c)
        else:
            arrived = from_z(c)
        if c + Z_FIRST < NC:
            over_z(c + Z_FIRST, back_left, back_right, from_plane(c + Z_FIRST))
        if c + Z_FIRST + 1 < NC:
            plane_first(c + Z_FIRST + 1)
        if c == 0:
            relay_prompt()
        if c == 2:
            relay_near(1, 1)
        if c == 3:
            relay_near(2, 3)
        if 0 < c <= Z_FIRST:
            use_from_plane(c - 1)
        if c == 5:
            bytes_of(raw.at[0], t_ssem.at[0], t_rsem.at[0]).wait_recv()
            sort_prompt(0)
        if c >= Z_FIRST:
            use(c, dot(place_left, arrived).astype(BF16), dot(place_right, arrived).astype(BF16))
        if c == 3:
            relay_near(4, 6)
        if c == 5:
            for h in range(HEADS):
                cross_head(h)

    @pl.when(w < NW - 1)
    def _():
        bytes_of(raw.at[0], t_ssem.at[0], t_rsem.at[0]).wait_send()

    @pl.when(w == NW - 1)
    def _():
        bytes_of(raw.at[0, pl.ds(0, 6 * PIECE)], t_ssem.at[1], t_rsem.at[1]).wait_send()
        bytes_of(raw.at[0, pl.ds(0, OWN_PIECE)], t_ssem.at[2], t_rsem.at[2]).wait_send()

    @pl.when(inner)
    def _():
        bytes_of(relay, t_ssem.at[2], t_rsem.at[2]).wait_send()
        bytes_of(near_relay, r_sems.at[0], r_sems.at[1]).wait_send()

    bytes_of(slot_send.at[pl.ds(0, NZ - 1)], s_sems.at[0], s_sems.at[1]).wait_send()
    bytes_of(row_recv.at[pl.ds(0, NW - 1)], s_sems.at[2], s_sems.at[3]).wait_send()
    for i in range(2):
        bytes_of(img_near.at[i], i_sems.at[2 * i], i_sems.at[2 * i + 1]).wait_send()
    for i, n in enumerate(near):
        for side in range(2):
            bytes_of(near_part(n, side), n_ssem.at[2 * i + side], n_rsem.at[2 * i + side]).wait_send()
    for c in range(NC):
        bytes_of(ybuf[c].at[pl.ds(0, 96)], y_ssem.at[c], y_rsem.at[c]).wait_send()
        bytes_of(zsend[c].at[pl.ds(0, NZ - 1)], z_ssem.at[c], z_rsem.at[c]).wait_send()
        bytes_of(xsend[c].at[pl.ds(0, NW - 1)], x_ssem.at[c], x_rsem.at[c]).wait_send()


def body(queries, keys, values, text_queries, text_states, packed_pos, image_of):
    dma = pltpu.SemaphoreType.DMA
    scratch = []
    scratch += [pltpu.VMEM((ROWS, n), BF16) for _, _, n in CHUNKS]
    scratch += [pltpu.VMEM((NZ, 16, n // 2), BF16) for _, _, n in CHUNKS] * 2
    scratch += [pltpu.VMEM((NW, NZ, n), BF16) for _, _, n in CHUNKS] * 2
    scratch += [
        pltpu.VMEM((2, ROWS, FEAT), BF16),
        pltpu.VMEM((2, 3 * ROWS, FEAT), BF16),
        pltpu.VMEM((PIECE, HD), BF16),
        pltpu.VMEM((ROWS, CHUNKS[0][2]), BF16),
        pltpu.VMEM((2, TXT_ROWS, HD), BF16),
        pltpu.VMEM((2, HEADS, 2, TXT_PAD, HD), BF16),
        pltpu.VMEM((ROWS, FEAT), F32),
        pltpu.VMEM((NZ, 1, ROWS), I32),
        pltpu.VMEM((NZ, 1, ROWS), I32),
        pltpu.VMEM((1, ROWS), I32),
        pltpu.VMEM((NW, 1, ROWS), I32),
        pltpu.VMEM((2, 1, ROWS), I32),
    ]
    scratch += [dma((NC + 1,))] + [dma((NC,))] * 6 + [dma((2 * NC,))] * 2 + [dma((4,))] * 4 + [dma((2,))]
    hbm = pl.BlockSpec(memory_space=pl.ANY)
    vmem = pl.BlockSpec(memory_space=pltpu.VMEM)
    prompt = text_states.transpose(1, 2, 0, 3).reshape(TXT, 2, HEADS, HD).transpose(0, 2, 1, 3).reshape(TXT_ROWS, HD)
    return pl.pallas_call(
        kernel,
        out_shape=jax.ShapeDtypeStruct((ROWS, FEAT), BF16),
        in_specs=[hbm] * 5 + [vmem] * 2,
        out_specs=vmem,
        scratch_shapes=scratch,
        compiler_params=pltpu.CompilerParams(collective_id=0, has_side_effects=True, vmem_limit_bytes=60 * 2**20),
    )(queries, keys, values, text_queries, prompt, packed_pos.reshape(1, ROWS), image_of.reshape(1, ROWS))


def solution(mesh):
    return jax.shard_map(
        body,
        mesh=mesh,
        in_specs=(
            P(("seq", "mp"), None),
            P(("seq", "mp"), None),
            P(("seq", "mp"), None),
            P(("seq", "mp"), None),
            P(None, "seq", None, "mp"),
            P("seq"),
            P("seq"),
        ),
        out_specs=P("seq", "mp"),
        check_vma=False,
    )
```
